256 devices in a mesh: dp: 16 (over x, y_hi, core), mp: 16 (over z, y_lo).
Axes of the slice: x: 4, y: 4 (y_hi: 2, y_lo: 2; y = y_hi * 2 + y_lo), z: 8, core: 2. Of those that a mesh axis runs over, the one named last changes fastest.
Arguments:
- tokens: bfloat16 [4096, 6144], P('dp', 'mp'), may hold values from -6 to 6
- ln_gain: bfloat16 [6144], replicated, may hold values from 0.25 to 1.75
- w_qkv: bfloat16 [6144, 32, 384], P(None, 'mp'), as said below
- q_gain: bfloat16 [128], replicated, may hold values from 0.25 to 1.75
- k_gain: bfloat16 [128], replicated, may hold values from 0.25 to 1.75
- d_out: bfloat16 [4096, 4096], P('dp', 'mp'), may hold values from -6 to 6
Outputs:
- attn_out: bfloat16 [4096, 4096], P('dp', 'mp')
- grad_tokens: bfloat16 [4096, 6144], P('dp', 'mp')
- grad_weight: float32 [6144, 32, 384], P('dp', 'mp')
The draws below stay inside these ranges and needn't reach their ends.
Inputs may be any that keep to these rules, and one draw needn't show every extreme that they name: `w_qkv`: entries of order 6144 ** -0.5.
All inputs are finite; a program needn't handle non-finite values.
Results may differ from the reference program's by a relative error of at most 0.028.
Values may be sent and summed in bfloat16 or wider, within the bound.
No kernel may reach another device: no remote copies, remote signals or barrier semaphores. Data moves between devices by JAX's collectives and lax.ppermute only.
A program may use at most 128 MiB of HBM per device.

```python
import math
import jax
import jax.numpy as jnp
from jax import lax

D = 6144
HEADS = 32
HEAD_DIM = 128
PATCHES = 256
TOKENS = 4096


def draw_w_qkv(key, part):
    key = jax.random.fold_in(key, 11)
    key_noise, key_column, key_phase, key_rough, key_pairs = jax.random.split(key, 5)
    width = 3 * HEAD_DIM
    positions = jnp.arange(D).astype(jnp.float32) / D
    phase = jax.random.uniform(key_phase, (), jnp.float32, 0.0, 2.0 * math.pi)
    noise = jax.random.normal(key_noise, (D, HEADS, width), jnp.float32)
    column = 0.4 * jax.random.normal(key_column, (HEADS, width), jnp.float32)
    rough = jax.random.uniform(key_rough, (D,), jnp.float32, 0.5, 1.5)
    profile = (1.6 + 1.2 * jnp.sin(2.0 * math.pi * positions + phase)) * rough
    pairing = jax.random.permutation(key_pairs, HEADS)
    block_ids = jnp.arange(D) // (D // HEADS)
    spike = jnp.where(block_ids[:, None] == pairing[None, :], 3.0, 1.0).astype(jnp.float32)
    values = noise * spike[:, :, None] + profile[:, None, None] * column[None, :, :]
    return (values * (1.5 * D) ** (-0.5)).astype(jnp.bfloat16)


def with_spikes(array, rng, source, target, parts, factor):
    def block_of(position):
        return (jnp.arange(array.shape[position]) // (array.shape[position] // parts)).reshape((-1,) + (1,) * (array.ndim - 1 - position))

    near = jax.random.permutation(rng, parts)[block_of(target)]
    second = (block_of(target) + parts // 2) % parts
    return jnp.where((block_of(source) == near) | (block_of(source) == second), factor * array, array)


def shard_levels(key, dims, cuts, least, high):
    level, own = 1.0, jax.random.fold_in(key, 6)
    for dim, shards_of in cuts:
        heights = jnp.exp(jax.random.uniform(jax.random.fold_in(own, dim), (shards_of,), jnp.float32, least / len(cuts), high / len(cuts)))
        level = level * jnp.repeat(heights, dims[dim] // shards_of).reshape([-1 if axis == dim else 1 for axis in range(len(dims))])
    return level


def normal_values(own_key, shape, spread, most, shards=(), kind=jnp.bfloat16):
    result = spread * jax.random.normal(own_key, shape, jnp.float32)
    if shards:
        result = result * shard_levels(own_key, shape, shards, -0.22, 0.18)
    return jnp.clip(result, -most, most).astype(kind)


def bell_draw_with(own_key, dims, scale, bound, shards, heavy, held_as=jnp.bfloat16):
    entries = scale * jax.random.normal(own_key, dims, jnp.float32)
    if shards:
        entries = entries * shard_levels(own_key, dims, shards, -0.22, 0.18)
    return jnp.clip(with_spikes(entries, jax.random.fold_in(own_key, 3), *heavy), -bound, bound).astype(held_as)


def setup_inputs(seed: int = 0) -> dict:
    seeds = jax.random.split(jax.random.key(seed), 7)
    tokens = bell_draw_with(seeds[0], (TOKENS, D), 1.0, 6.0, ((0, 16), (1, 16)), (0, 1, 16, 2.0))
    ln_gain = jnp.clip(1.0 + 0.15 * jax.random.normal(seeds[1], (D,), jnp.float32), 0.25, 1.75).astype(jnp.bfloat16)
    w_qkv = draw_w_qkv(jax.random.fold_in(seeds[6], 71), 0)
    q_gain = jnp.clip(1.0 + 0.15 * jax.random.normal(seeds[3], (HEAD_DIM,), jnp.float32), 0.25, 1.75).astype(jnp.bfloat16)
    k_gain = jnp.clip(1.0 + 0.15 * jax.random.normal(seeds[4], (HEAD_DIM,), jnp.float32), 0.25, 1.75).astype(jnp.bfloat16)
    d_out = normal_values(seeds[5], (TOKENS, HEADS * HEAD_DIM), 1.0, 6.0, ((0, 16), (1, 16)))
    return {"tokens": tokens, "ln_gain": ln_gain, "w_qkv": w_qkv, "q_gain": q_gain, "k_gain": k_gain, "d_out": d_out}


EPSILON = 1e-06

def halve(values):
    return lax.optimization_barrier(values.astype(jnp.bfloat16))

def mix(form, left, right):
    return jnp.einsum(form, left.astype(jnp.float32), right.astype(jnp.float32))

def head_norm(values, norm_gain):
    avg_vals = lax.optimization_barrier(jnp.mean(values, -1, keepdims=True))
    centred = values - avg_vals
    inv_std = lax.rsqrt(lax.optimization_barrier(jnp.mean(centred * centred, -1, keepdims=True)) + EPSILON)
    unit_vals = centred * inv_std
    return (unit_vals * norm_gain.astype(jnp.float32), unit_vals, inv_std)

def norm_back(grad_vals, norm_gain, unit_vals, inv_std):
    scaled = grad_vals * norm_gain.astype(jnp.float32)
    return inv_std * (scaled - lax.optimization_barrier(jnp.mean(scaled, -1, keepdims=True)) - unit_vals * lax.optimization_barrier(jnp.mean(scaled * unit_vals, -1, keepdims=True)))

def attend(qkv, q_gain, k_gain, d_out, patch_count):
    row_count, head_count, qkv_width = qkv.shape
    head_width = qkv_width // 3
    image_count = row_count // patch_count
    per_image = qkv.reshape(image_count, patch_count, head_count, qkv_width)
    q_normed, q_unit, q_inv = head_norm(per_image[..., :head_width], q_gain)
    k_normed, k_unit, k_inv = head_norm(per_image[..., head_width:2 * head_width], k_gain)
    q_half = halve(q_normed)
    k_half = halve(k_normed)
    v_half = halve(per_image[..., 2 * head_width:])
    score_scale = head_width ** (-0.5)
    scores = mix('iphd,iqhd->ihpq', q_half, k_half) * score_scale
    exp_scores = jnp.exp(scores)
    attn_probs = exp_scores / lax.optimization_barrier(jnp.sum(exp_scores, -1, keepdims=True))
    probs_half = halve(attn_probs)
    attn_out = mix('ihpq,iqhd->iphd', probs_half, v_half).astype(jnp.bfloat16)
    grad_out = d_out.reshape(image_count, patch_count, head_count, head_width)
    grad_probs = mix('iphd,iqhd->ihpq', grad_out, v_half)
    grad_value = mix('ihpq,iphd->iqhd', probs_half, grad_out)
    grad_scores = attn_probs * (grad_probs - lax.optimization_barrier(jnp.sum(attn_probs * grad_probs, -1, keepdims=True))) * score_scale
    grad_half = halve(grad_scores)
    grad_qnorm = mix('ihpq,iqhd->iphd', grad_half, k_half)
    grad_knorm = mix('ihpq,iphd->iqhd', grad_half, q_half)
    grad_query = norm_back(grad_qnorm, q_gain, q_unit, q_inv)
    grad_key = norm_back(grad_knorm, k_gain, k_unit, k_inv)
    grad_qkv = jnp.concatenate([grad_query, grad_key, grad_value], -1).astype(jnp.bfloat16)
    return (attn_out.reshape(row_count, head_count * head_width), grad_qkv.reshape(row_count, head_count, qkv_width))

def reference(tokens, ln_gain, w_qkv, q_gain, k_gain, d_out):
    row_count = tokens.shape[0]
    tok_wide = tokens.astype(jnp.float32)
    gain_wide = ln_gain.astype(jnp.float32)
    row_mean = lax.optimization_barrier(jnp.sum(tok_wide, 1, keepdims=True)) / D
    row_var = lax.optimization_barrier(jnp.sum(tok_wide * tok_wide, 1, keepdims=True)) / D - row_mean * row_mean
    inv_std = lax.rsqrt(row_var + EPSILON)
    unit_rows = (tok_wide - row_mean) * inv_std
    normed = (unit_rows * gain_wide).astype(jnp.bfloat16)
    qkv_width = w_qkv.shape[2]
    flat_w = w_qkv.reshape(D, HEADS * qkv_width)
    qkv = jnp.dot(normed, flat_w, preferred_element_type=jnp.float32).reshape(row_count, HEADS, qkv_width)
    attn_out, grad_qkv = attend(qkv, q_gain, k_gain, d_out, PATCHES)
    grad_flat = grad_qkv.reshape(row_count, HEADS * qkv_width)
    grad_normed = lax.dot_general(grad_flat, flat_w, (((1,), (1,)), ((), ())), preferred_element_type=jnp.float32)
    scaled = grad_normed * gain_wide
    mean_scaled = lax.optimization_barrier(jnp.sum(scaled, 1, keepdims=True)) / D
    mean_cross = lax.optimization_barrier(jnp.sum(scaled * unit_rows, 1, keepdims=True)) / D
    grad_tokens = (inv_std * (scaled - mean_scaled - unit_rows * mean_cross)).astype(jnp.bfloat16)
    grad_weight = lax.dot_general(normed, grad_flat, (((0,), (0,)), ((), ())), preferred_element_type=jnp.float32)
    return (attn_out, grad_tokens, grad_weight.reshape(D, HEADS, qkv_width))
```

```python
import functools
import jax
import jax.numpy as jnp
from jax import lax
from jax.experimental import pallas as pl
from jax.experimental.pallas import tpu as pltpu
from jax.sharding import PartitionSpec as P

EPSILON = 1e-06
Z, YL, X, YH, CORES = 8, 2, 4, 2, 2
BF, F32 = jnp.bfloat16, jnp.float32
MIB = 1 << 20


def z_step(values, d):
    pairs = [(z * YL + y, ((z + d) % Z) * YL + y) for z in range(Z) for y in range(YL)]
    return lax.ppermute(values, "mp", pairs)


def yl_swap(values):
    return lax.ppermute(values, "mp", [(i, i ^ 1) for i in range(Z * YL)])


def x_step(values, d):
    n = YH * CORES
    pairs = [(x * n + r, ((x + d) % X) * n + r) for x in range(X) for r in range(n)]
    return lax.ppermute(values, "dp", pairs)


def yh_swap(values):
    return lax.ppermute(values, "dp", [(i, i ^ 2) for i in range(X * YH * CORES)])


def core_swap(values):
    return lax.ppermute(values, "dp", [(i, i ^ 1) for i in range(X * YH * CORES)])


def cost(flops, nbytes):
    return pl.CostEstimate(flops=flops, bytes_accessed=nbytes, transcendentals=0)


def gather_tokens(tokens):
    half = tokens.shape[0] // 2
    up, low = tokens[:half], tokens[half:]
    low_own = {0: low}
    low_own[Z - 1] = z_step(low, 1)
    low_own[1] = z_step(low, -1)
    up_other = yl_swap(up)
    upper = {0: jnp.stack([up, up_other])}
    low_other = {0: yl_swap(low)}
    for s in range(1, Z // 2):
        upper[Z - s] = z_step(upper[(Z - s + 1) % Z], 1)
        upper[s] = z_step(upper[s - 1], -1)
        if s > 1:
            low_own[Z - s] = z_step(low_own[Z - s + 1], 1)
            low_own[s] = z_step(low_own[s - 1], -1)
    far = Z // 2
    quarter = half // 2
    upper[far] = jnp.stack([z_step(upper[far + 1][0], 1), z_step(upper[far - 1][1], -1)])
    low_own[far] = jnp.concatenate(
        [z_step(low_own[far + 1][:quarter], 1), z_step(low_own[far - 1][quarter:], -1)]
    )
    for s in range(1, far):
        both = yl_swap(jnp.stack([low_own[Z - s], low_own[s]]))
        low_other[Z - s], low_other[s] = both[0], both[1]
    low_other[far] = yl_swap(low_own[far])
    return upper, low_own, low_other


def project_kernel(pos, *refs):
    ups, lows_own, lows_other = refs[:Z], refs[Z : 2 * Z], refs[2 * Z : 3 * Z]
    gain_ref, w_ref, qkv_ref, wg_ref, own_ref, sib_ref, mean_ref, inv_ref = refs[3 * Z :]
    step = pl.program_id(0)
    z0, yl, core = pos[0], pos[1], pos[2]
    half, width = lows_own[0].shape
    cols = width * YL * Z

    @pl.when(step == 0)
    def _():
        for top in (True, False):
            total = jnp.zeros((half, 1), F32)
            square = jnp.zeros((half, 1), F32)
            acc = jnp.zeros((half, width), F32)
            acc2 = jnp.zeros((half, width), F32)
            for d in range(Z):
                for r in range(YL):
                    if top:
                        v = ups[d][r]
                    else:
                        v = (lows_own if r == 0 else lows_other)[d][...]
                    v = v.astype(F32)
                    acc = acc + v
                    acc2 = acc2 + v * v
            total = jnp.sum(acc, 1, keepdims=True)
            square = jnp.sum(acc2, 1, keepdims=True)
            mean = total / cols
            inv = lax.rsqrt(square / cols - mean * mean + EPSILON)
            rows = pl.ds(0 if top else half, half)
            mean_ref[rows, :] = mean
            inv_ref[rows, :] = inv
        qkv_ref[...] = jnp.zeros_like(qkv_ref)
        wg_ref[...] = jnp.zeros_like(wg_ref)

    for d in range(Z):

        @pl.when(step == d)
        def _():
            zd = lax.rem(z0 + d, Z)
            for r in range(YL):
                y = yl if r == 0 else 1 - yl
                gain = gain_ref[zd * YL + y]
                low = (lows_own if r == 0 else lows_other)[d]
                parts = []
                for top in (True, False):
                    v = (ups[d][r] if top else low[...]).astype(F32)
                    rows = pl.ds(0 if top else half, half)
                    v = (v - mean_ref[rows, :]) * inv_ref[rows, :] * gain
                    parts.append(v.astype(BF))
                normed = jnp.concatenate(parts, 0)

                @pl.when(y == core)
                def _():
                    own_ref[zd] = normed

                @pl.when(y != core)
                def _():
                    sib_ref[zd] = normed

                w = w_ref[0, y]
                qkv_ref[...] += jnp.dot(normed, w, preferred_element_type=F32)
                gains = jnp.broadcast_to(gain, (16, width)).astype(BF)
                wg_ref[...] += jnp.dot(gains, w, preferred_element_type=F32)


def project(pos, upper, low_own, low_other, gain, w):
    half, width = low_own[0].shape
    n = w.shape[-1]
    rows = 2 * half
    whole = lambda a: pl.BlockSpec(a.shape, lambda s, p: (0,) * a.ndim)
    pieces = [upper[d] for d in range(Z)] + [low_own[d] for d in range(Z)] + [low_other[d] for d in range(Z)]
    gain = gain.reshape(Z * YL, 1, width)
    blocks = jax.ShapeDtypeStruct((Z, rows, width), BF)
    return pl.pallas_call(
        project_kernel,
        grid_spec=pltpu.PrefetchScalarGridSpec(
            num_scalar_prefetch=1,
            grid=(Z,),
            in_specs=[whole(a) for a in pieces]
            + [
                whole(gain),
                pl.BlockSpec((1, YL, width, n), lambda s, p: (lax.rem(p[0] + s, Z), 0, 0, 0)),
            ],
            out_specs=[
                pl.BlockSpec((rows, n), lambda s, p: (0, 0)),
                pl.BlockSpec((16, n), lambda s, p: (0, 0)),
                pl.BlockSpec((Z, rows, width), lambda s, p: (0, 0, 0)),
                pl.BlockSpec((Z, rows, width), lambda s, p: (0, 0, 0)),
                pl.BlockSpec((rows, 1), lambda s, p: (0, 0)),
                pl.BlockSpec((rows, 1), lambda s, p: (0, 0)),
            ],
        ),
        out_shape=[
            jax.ShapeDtypeStruct((rows, n), F32),
            jax.ShapeDtypeStruct((16, n), F32),
            blocks,
            blocks,
            jax.ShapeDtypeStruct((rows, 1), F32),
            jax.ShapeDtypeStruct((rows, 1), F32),
        ],
        compiler_params=pltpu.CompilerParams(vmem_limit_bytes=32 * MIB),
        cost_estimate=cost(2 * rows * width * Z * YL * n, 2 * width * Z * YL * n),
        name="project",
    )(pos, *pieces, gain, w.reshape(Z, YL, width, n))


def dot_nt(a, b):
    return lax.dot_general(a, b, (((1,), (1,)), ((), ())), preferred_element_type=F32)


def dot_tn(a, b):
    return lax.dot_general(a, b, (((0,), (0,)), ((), ())), preferred_element_type=F32)


def dot_nn(a, b):
    return jnp.dot(a, b, preferred_element_type=F32)


def head_norm(values):
    centred = values - jnp.mean(values, -1, keepdims=True)
    inv = lax.rsqrt(jnp.mean(centred * centred, -1, keepdims=True) + EPSILON)
    return centred * inv, inv


def norm_back(grad, gain, unit, inv):
    scaled = grad * gain
    return inv * (
        scaled
        - jnp.mean(scaled, -1, keepdims=True)
        - unit * jnp.mean(scaled * unit, -1, keepdims=True)
    )


def attend_kernel(heads, hd, qkv_ref, wg_ref, qg_ref, kg_ref, do_ref, out_ref, gq_ref, sums_ref):
    scale = hd ** (-0.5)
    q_gain, k_gain = qg_ref[...], kg_ref[...]
    rows = qkv_ref.shape[0]
    acc_sum = jnp.zeros((rows, hd), F32)
    acc_cross = jnp.zeros((rows, hd), F32)
    for h in range(heads):
        base = h * 3 * hd
        q, k, v = (qkv_ref[:, base + i * hd : base + (i + 1) * hd] for i in range(3))
        q_unit, q_inv = head_norm(q)
        k_unit, k_inv = head_norm(k)
        q_half = (q_unit * q_gain).astype(BF)
        k_half = (k_unit * k_gain).astype(BF)
        v_half = v.astype(BF)
        d_out = do_ref[:, h * hd : (h + 1) * hd]
        exps = jnp.exp(dot_nt(q_half, k_half) * scale)
        probs = exps / jnp.sum(exps, -1, keepdims=True)
        probs_half = probs.astype(BF)
        out_ref[:, h * hd : (h + 1) * hd] = dot_nn(probs_half, v_half).astype(BF)
        grad_probs = dot_nt(d_out, v_half)
        grad_value = dot_tn(probs_half, d_out)
        inner = jnp.sum(probs * grad_probs, -1, keepdims=True)
        grad_scores = (probs * (grad_probs - inner) * scale).astype(BF)
        grad_q = norm_back(dot_nn(grad_scores, k_half), q_gain, q_unit, q_inv)
        grad_k = norm_back(dot_tn(grad_scores, q_half), k_gain, k_unit, k_inv)
        for i, (part, source) in enumerate(((grad_q, q), (grad_k, k), (grad_value, v))):
            cols = slice(base + i * hd, base + (i + 1) * hd)
            half = part.astype(BF)
            gq_ref[:, cols] = half
            wide = half.astype(F32)
            acc_sum = acc_sum + wide * wg_ref[0:1, cols]
            acc_cross = acc_cross + wide * source
    sums = jnp.sum(acc_sum, -1, keepdims=True)
    cross = jnp.sum(acc_cross, -1, keepdims=True)
    lane = lax.broadcasted_iota(jnp.int32, (rows, hd), 1)
    both = jnp.where(lane == 0, sums, jnp.where(lane == 1, cross, 0.0))
    sums_ref[...] = both.T[:8]


def attend(qkv, wg, q_gain, k_gain, d_out, hd):
    rows, n = qkv.shape
    heads = n // (3 * hd)
    return pl.pallas_call(
        functools.partial(attend_kernel, heads, hd),
        out_shape=[
            jax.ShapeDtypeStruct((rows, heads * hd), BF),
            jax.ShapeDtypeStruct((rows, n), BF),
            jax.ShapeDtypeStruct((8, rows), F32),
        ],
        compiler_params=pltpu.CompilerParams(vmem_limit_bytes=24 * MIB),
        cost_estimate=cost(14 * heads * rows * rows * hd, 4 * rows * n),
        name="attend",
    )(qkv, wg, q_gain.astype(F32).reshape(1, hd), k_gain.astype(F32).reshape(1, hd), d_out)


def token_kernel(pos, gq_ref, w_ref, out_ref):
    out_ref[0] = dot_nt(gq_ref[...], w_ref[0]).astype(BF)


def token_terms(blocks, gq, w):
    rows, n = gq.shape
    wide = w.shape[1]
    count = blocks.shape[0]
    return pl.pallas_call(
        token_kernel,
        grid_spec=pltpu.PrefetchScalarGridSpec(
            num_scalar_prefetch=1,
            grid=(count,),
            in_specs=[
                pl.BlockSpec((rows, n), lambda s, p: (0, 0)),
                pl.BlockSpec((1, wide, n), lambda s, p: (p[s], 0, 0)),
            ],
            out_specs=pl.BlockSpec((1, rows, wide), lambda s, p: (s, 0, 0)),
        ),
        out_shape=jax.ShapeDtypeStruct((count, rows, wide), BF),
        compiler_params=pltpu.CompilerParams(vmem_limit_bytes=16 * MIB),
        cost_estimate=cost(2 * count * rows * wide * n, 2 * count * wide * n),
        name="token_terms",
    )(blocks, gq, w)


def weight_kernel(pos, own_ref, sib_ref, gq_ref, gs_ref, out_ref):
    out_ref[0] = (dot_tn(own_ref[0], gq_ref[...]) + dot_tn(sib_ref[0], gs_ref[...])).astype(BF)


def weight_terms(blocks, own, sib, gq, gs, width, at):
    rows, n = gq.shape
    count = blocks.shape[0]
    piece = pl.BlockSpec((1, rows, width), lambda s, p: (p[s], 0, at))
    flat = pl.BlockSpec((rows, n), lambda s, p: (0, 0))
    return pl.pallas_call(
        weight_kernel,
        grid_spec=pltpu.PrefetchScalarGridSpec(
            num_scalar_prefetch=1,
            grid=(count,),
            in_specs=[piece, piece, flat, flat],
            out_specs=pl.BlockSpec((1, width, n), lambda s, p: (s, 0, 0)),
        ),
        out_shape=jax.ShapeDtypeStruct((count, width, n), BF),
        compiler_params=pltpu.CompilerParams(vmem_limit_bytes=16 * MIB),
        cost_estimate=cost(4 * count * rows * width * n, 2 * count * width * n),
        name="weight_terms",
    )(blocks, own, sib, gq, gs)


def add(*terms):
    total = terms[0].astype(F32)
    for term in terms[1:]:
        total = total + term.astype(F32)
    return total.astype(BF)


def local(tokens, ln_gain, w_qkv, q_gain, k_gain, d_out):
    rows, width = tokens.shape
    cols = width * Z * YL
    heads, n3 = w_qkv.shape[1:]
    n = heads * n3
    hd = n3 // 3
    mp, dp = lax.axis_index("mp"), lax.axis_index("dp")
    z0, yl = mp // YL, mp % YL
    x0, yh, core = dp // (YH * CORES), dp // CORES % YH, dp % CORES
    pos = jnp.stack([z0, yl, core]).astype(jnp.int32)
    w = w_qkv.reshape(cols, n)

    with jax.named_scope("gather"):
        upper, low_own, low_other = gather_tokens(tokens)
    gain = ln_gain.astype(F32)
    qkv, wg, own, for_sib, mean, inv = project(pos, upper, low_own, low_other, gain, w)
    with jax.named_scope("core_rows"):
        sib = core_swap(for_sib)
    attn_out, gq, sums = attend(qkv, wg, q_gain, k_gain, d_out, hd)
    with jax.named_scope("core_grads"):
        gs = core_swap(gq)

    with jax.named_scope("sums"):
        for step in (yl_swap, *(functools.partial(z_step, d=d) for d in (1, 2, 4))):
            sums = sums + step(sums)

    wz = w.reshape(Z, width * YL, n)
    at = lambda *ds: jnp.stack([(z0 + d) % Z for d in ds]).astype(jnp.int32)
    far = Z // 2
    first = token_terms(at(far), gq, wz)[0]
    block = lambda dx, h: ((x0 + dx) % X) * YH + h
    ids = lambda *items: jnp.stack([block(dx, h) for dx, h in items]).astype(jnp.int32)
    main, rest = 2 * width // 3, width // 3
    with jax.named_scope("z_relay1"):
        fwd = z_step(first[:, :width], 1)
        bwd = z_step(first[:, width:], -1)
    weight_main = lambda *items: weight_terms(ids(*items), own, sib, gq, gs, main, 0)
    weight_rest = lambda *items: weight_terms(ids(*items), own, sib, gq, gs, rest, 2)
    w_far = weight_main((2, 0), (2, 1))
    with jax.named_scope("x_relay1"):
        w_fwd = x_step(w_far[0], 1)
        w_bwd = x_step(w_far[1], -1)
    r_other = weight_rest(*((dx, 1 - yh) for dx in (2, 1, 3, 0)))
    with jax.named_scope("yh_rest"):
        r_got = yh_swap(r_other)
    terms = token_terms(at(3, 5, 2, 6, 1, 7, 0), gq, wz)
    w_near = weight_main((1, 0), (1, 1), (3, 0), (3, 1), (0, 0), (0, 1))
    r_own = weight_rest(*((dx, yh) for dx in (2, 1, 3, 0)))

    with jax.named_scope("z_relay2"):
        fwd = z_step(jnp.concatenate([add(terms[0][:, :width], fwd), terms[0][:, width:]], 1), 1)
        bwd = z_step(jnp.concatenate([terms[1][:, :width], add(terms[1][:, width:], bwd)], 1), -1)
    with jax.named_scope("x_relay2"):
        w_fwd = x_step(jnp.stack([add(w_near[0], w_fwd), w_near[1]]), 1)
        w_bwd = x_step(jnp.stack([w_near[2], add(w_near[3], w_bwd)]), -1)
    with jax.named_scope("z_relay3"):
        fwd = z_step(add(terms[2], fwd), 1)
        bwd = z_step(add(terms[3], bwd), -1)
    r_sum = add(r_own, r_got)
    cut = rest // 2
    with jax.named_scope("z_relay4"):
        fwd = z_step(add(terms[4], fwd), 1)
        bwd = z_step(add(terms[5], bwd), -1)
    with jax.named_scope("x_rest1"):
        r_fwd = x_step(r_sum[0][:cut], 1)
        r_bwd = x_step(r_sum[0][cut:], -1)
    with jax.named_scope("x_rest2"):
        r_fwd = x_step(jnp.concatenate([add(r_sum[1][:cut], r_fwd), r_sum[1][cut:]]), 1)
        r_bwd = x_step(jnp.concatenate([r_sum[2][:cut], add(r_sum[2][cut:], r_bwd)]), -1)

    pick = lambda a, i: lax.dynamic_index_in_dim(a, i, 0, keepdims=False)
    with jax.named_scope("y_tokens"):
        halves = [[a[:, :width], a[:, width:]] for a in (terms[6], fwd, bwd)]
        lows = [h[0] for h in halves]
        highs = [h[1] for h in halves]
        low_sum, high_sum = add(*lows), add(*highs)
        mine = jnp.where(yl == 0, low_sum, high_sum)
        other = yl_swap(jnp.where(yl == 0, high_sum, low_sum))
        grad_normed = mine.astype(F32) + other.astype(F32)
        own_gain = lax.dynamic_slice_in_dim(gain, mp * width, width)
        unit = (tokens.astype(F32) - mean) * inv
        scaled = grad_normed * own_gain
        grad_tokens = (
            inv * (scaled - sums[0][:, None] / cols - unit * (sums[1][:, None] / cols))
        ).astype(BF)
    with jax.named_scope("y_weight"):
        both = [w_near[4:6], w_fwd, w_bwd]
        got = yh_swap(add(*(pick(b, 1 - yh) for b in both)))
        w_main = sum(pick(b, yh).astype(F32) for b in both) + got.astype(F32)
        w_rest = r_sum[3].astype(F32) + r_fwd.astype(F32) + r_bwd.astype(F32)
        grad_weight = jnp.concatenate([w_main, w_rest]).reshape(width, heads, n3)
    return attn_out, grad_tokens, grad_weight


def solution(mesh):
    in_specs = (P("dp", "mp"), P(), P(None, "mp", None), P(), P(), P("dp", "mp"))
    out_specs = (P("dp", "mp"), P("dp", "mp"), P("dp", "mp", None))
    return jax.shard_map(local, mesh=mesh, in_specs=in_specs, out_specs=out_specs, check_vma=False)
```

```python
import functools
import jax
import jax.numpy as jnp
from jax import lax
from jax.experimental import pallas as pl
from jax.experimental.pallas import tpu as pltpu
from jax.sharding import PartitionSpec as P

EPSILON = 1e-06
Z, YL, X, YH, CORES = 8, 2, 4, 2, 2
BF, F32 = jnp.bfloat16, jnp.float32
MIB = 1 << 20
GROUP = 16
EXTRA = 16
FAR = Z // 2
COST = pl.CostEstimate(flops=1024, bytes_accessed=1024, transcendentals=0)


def z_step(values, d):
    pairs = [(z * YL + y, ((z + d) % Z) * YL + y) for z in range(Z) for y in range(YL)]
    return lax.ppermute(values, "mp", pairs)


def yl_swap(values):
    return lax.ppermute(values, "mp", [(i, i ^ 1) for i in range(Z * YL)])


def x_step(values, d):
    n = YH * CORES
    pairs = [(x * n + r, ((x + d) % X) * n + r) for x in range(X) for r in range(n)]
    return lax.ppermute(values, "dp", pairs)


def yh_swap(values):
    return lax.ppermute(values, "dp", [(i, i ^ 2) for i in range(X * YH * CORES)])


def core_swap(values):
    return lax.ppermute(values, "dp", [(i, i ^ 1) for i in range(X * YH * CORES)])


def z_index():
    return lax.axis_index("mp") // YL


def yl_index():
    return lax.rem(lax.axis_index("mp"), YL)


def x_index():
    return lax.axis_index("dp") // (YH * CORES)


def yh_index():
    return lax.rem(lax.axis_index("dp") // CORES, YH)


def core_index():
    return lax.rem(lax.axis_index("dp"), CORES)


def held(shape, dtype):
    return pltpu.VMEM(shape, dtype)


def call(kernel, out_shape, *args, deps=(), hbm=(), limit=6, scratch=()):
    vmem, anywhere = pl.BlockSpec(memory_space=pltpu.VMEM), pl.BlockSpec(memory_space=pl.ANY)
    specs = [anywhere if i in hbm else vmem for i in range(len(args))]
    count = len(args)
    name = getattr(kernel, "func", kernel).__name__

    def body(*refs):
        kernel(*refs[:count], *refs[count + len(deps) :])

    return pl.pallas_call(
        body,
        in_specs=specs + [anywhere] * len(deps),
        out_specs=[vmem] * len(out_shape),
        out_shape=[(jax.ShapeDtypeStruct if o[2:] else held)(o[0], o[1]) for o in out_shape],
        scratch_shapes=list(scratch),
        compiler_params=pltpu.CompilerParams(vmem_limit_bytes=limit * MIB),
        cost_estimate=COST,
        name=name,
    )(*args, *deps)


def tie(value, dep):
    anywhere = pl.BlockSpec(memory_space=pl.ANY)
    return pl.pallas_call(
        lambda *refs: None,
        in_specs=[anywhere] * 2,
        out_specs=anywhere,
        out_shape=jax.ShapeDtypeStruct(value.shape, value.dtype),
        input_output_aliases={0: 0},
        compiler_params=pltpu.CompilerParams(vmem_limit_bytes=MIB),
        cost_estimate=COST,
        name="tie",
    )(value, dep)


def hold(ref, out_ref):
    out_ref[...] = ref[...]


def pair(own_ref, other_ref, out_ref):
    out_ref[0] = own_ref[...]
    out_ref[1] = other_ref[...]


def take(i, ref, out_ref):
    out_ref[...] = ref[i]


def load(w_hbm, out_ref, sems):
    groups = out_ref.shape[0] // Z
    copies = []
    for i in range(Z):
        part = pl.ds(i * groups, groups)
        copies.append(pltpu.make_async_copy(w_hbm.at[part], out_ref.at[part], sems.at[i]))
        copies[-1].start()
    for copy in copies:
        copy.wait()


def gather_tokens(tokens, w_qkv, *early):
    other = yl_swap(tokens)
    tokens = call(hold, [(tokens.shape, BF)], tokens, deps=early)[0]
    blocks = {0: call(pair, [((YL, *tokens.shape), BF)], tokens, other)[0]}
    w = w_qkv.reshape(-1, GROUP, *w_qkv.shape[1:]).swapaxes(1, 2)
    for s in range(1, FAR):
        blocks[Z - s] = z_step(blocks[(Z - s + 1) % Z], 1)
        blocks[s] = z_step(blocks[s - 1], -1)
        if s == 1:
            blocks[s] = tie(blocks[s], w[0, 0])
        if s == 2:
            kernel_shape, sems = [(w.shape, BF)], [pltpu.SemaphoreType.DMA((Z,))]
            w = call(load, kernel_shape, w, deps=[blocks[1]], hbm=[0], limit=46, scratch=sems)[0]
            blocks[s] = tie(blocks[s], w)
    half = [(tokens.shape, BF)]
    up = call(functools.partial(take, 0), half, blocks[FAR + 1])[0]
    down = call(functools.partial(take, 1), half, blocks[FAR - 1])[0]
    last = [z_step(up, 1), z_step(down, -1)]
    return [blocks[d] for d in range(Z) if d != FAR] + last, w, tokens


def joined(w_ref):
    heads, columns = w_ref.shape[1], w_ref.shape[3]
    return jnp.concatenate([w_ref[:, h].reshape(-1, columns) for h in range(heads)], 1)


def pair_at(refs, d):
    if d == FAR:
        return refs[-2][...], refs[-1][...]
    ref = refs[d if d < FAR else d - 1]
    return ref[0], ref[1]


def project(*refs):
    blocks = refs[: Z + 1]
    gain_ref, w_ref, qkv_ref, wg_ref, own_ref, sib_ref, stats_ref = refs[Z + 1 :]
    z0, yl, core = z_index(), yl_index(), core_index()
    rows, width = blocks[-1].shape
    cols = width * YL * Z

    acc = jnp.zeros((rows, width), F32)
    acc2 = jnp.zeros((rows, width), F32)
    for d in range(Z):
        for v in pair_at(blocks, d):
            v = v.astype(F32)
            acc = acc + v
            acc2 = acc2 + v * v
    mean = jnp.sum(acc, 1, keepdims=True) / cols
    square = jnp.sum(acc2, 1, keepdims=True) / cols
    inv = lax.rsqrt(square - mean * mean + EPSILON)
    lane = lax.broadcasted_iota(jnp.int32, (rows, 128), 1)
    stats_ref[...] = jnp.where(lane == 0, mean, jnp.where(lane == 1, inv, 0.0)).T[:8]
    qkv_ref[...] = jnp.zeros_like(qkv_ref)
    wg_ref[...] = jnp.zeros_like(wg_ref)
    groups = w_ref.shape[0] // (Z * YL)

    for d in range(Z):
        zd = lax.rem(z0 + d, Z)
        ys = (yl, 1 - yl)
        gains = [gain_ref[zd * YL + y] for y in ys]
        parts = [
            ((v.astype(F32) - mean) * inv * g).astype(BF) for v, g in zip(pair_at(blocks, d), gains)
        ]
        own_ref[zd] = jnp.where(core == yl, parts[0], parts[1])
        sib_ref[zd] = jnp.where(core == yl, parts[1], parts[0])
        extra = jnp.broadcast_to(jnp.concatenate(gains, 1), (16, width * YL)).astype(BF)
        left = jnp.concatenate([jnp.concatenate(parts, 1), extra], 0)
        firsts = [(zd * YL + y) * groups for y in ys]
        right = jnp.concatenate([joined(w_ref.at[pl.ds(f, groups)]) for f in firsts], 0)
        product = jnp.dot(left, right, preferred_element_type=F32)
        qkv_ref[...] += product[:rows]
        wg_ref[...] += product[rows:]


def dot_nt(a, b):
    return lax.dot_general(a, b, (((1,), (1,)), ((), ())), preferred_element_type=F32)


def dot_tn(a, b):
    return lax.dot_general(a, b, (((0,), (0,)), ((), ())), preferred_element_type=F32)


def dot_nn(a, b):
    return jnp.dot(a, b, preferred_element_type=F32)


def head_norm(values):
    centred = values - jnp.mean(values, -1, keepdims=True)
    inv = lax.rsqrt(jnp.mean(centred * centred, -1, keepdims=True) + EPSILON)
    return centred * inv, inv


def norm_back(grad, gain, unit, inv):
    scaled = grad * gain
    return inv * (
        scaled
        - jnp.mean(scaled, -1, keepdims=True)
        - unit * jnp.mean(scaled * unit, -1, keepdims=True)
    )


def pack(sums):
    high = sums.astype(BF).astype(F32)
    return jnp.concatenate([high, sums - high], 0).astype(BF)


def unpack(extra):
    wide = extra.astype(F32)
    half = wide.shape[0] // 2
    return wide[:half] + wide[half:]


def attend(heads, hd, qkv_ref, wg_ref, gains_ref, do_ref, w_ref, *outs):
    out_ref, gt_ref, sums_ref, fwd_ref, bwd_ref = outs
    scale = hd ** (-0.5)
    q_gain, k_gain = gains_ref[0:1], gains_ref[1:2]
    rows = qkv_ref.shape[0]
    acc_sum = jnp.zeros((rows, hd), F32)
    acc_cross = jnp.zeros((rows, hd), F32)
    for h in range(heads):
        base = h * 3 * hd
        q, k, v = (qkv_ref[:, base + i * hd : base + (i + 1) * hd] for i in range(3))
        q_unit, q_inv = head_norm(q)
        k_unit, k_inv = head_norm(k)
        q_half = (q_unit * q_gain).astype(BF)
        k_half = (k_unit * k_gain).astype(BF)
        v_half = v.astype(BF)
        d_out = do_ref[:, h * hd : (h + 1) * hd]
        exps = jnp.exp(dot_nt(q_half, k_half) * scale)
        probs = exps / jnp.sum(exps, -1, keepdims=True)
        probs_half = probs.astype(BF)
        out_ref[:, h * hd : (h + 1) * hd] = dot_nn(probs_half, v_half).astype(BF)
        grad_probs = dot_nt(d_out, v_half)
        grad_value = dot_tn(probs_half, d_out)
        inner = jnp.sum(probs * grad_probs, -1, keepdims=True)
        grad_scores = (probs * (grad_probs - inner) * scale).astype(BF)
        grad_q = norm_back(dot_nn(grad_scores, k_half), q_gain, q_unit, q_inv)
        grad_k = norm_back(dot_tn(grad_scores, q_half), k_gain, k_unit, k_inv)
        for i, (part, source) in enumerate(((grad_q, q), (grad_k, k), (grad_value, v))):
            cols = slice(base + i * hd, base + (i + 1) * hd)
            half = part.astype(BF)
            gt_ref[cols, :] = half.T
            wide = half.astype(F32)
            acc_sum = acc_sum + wide * wg_ref[0:1, cols]
            acc_cross = acc_cross + wide * source
    sums = jnp.sum(acc_sum, -1, keepdims=True)
    cross = jnp.sum(acc_cross, -1, keepdims=True)
    lane = lax.broadcasted_iota(jnp.int32, (rows, hd), 1)
    both = jnp.where(lane == 0, sums, jnp.where(lane == 1, cross, 0.0))
    sums = both.T[:8]
    sums_ref[...] = sums
    extra = pack(sums)
    width = fwd_ref.shape[0] - extra.shape[0]
    term = term_at(w_ref, gt_ref, FAR)
    for ref, part in ((fwd_ref, term[:width]), (bwd_ref, term[width:])):
        ref[:width] = part
        ref[width:] = extra


def term_at(w_ref, gt_ref, d):
    groups = w_ref.shape[0] // Z
    start = lax.rem(z_index() + d, Z) * groups
    return dot_nn(joined(w_ref.at[pl.ds(start, groups)]), gt_ref[...]).astype(BF)


def token_terms(distances, gt_ref, w_ref, out_ref):
    for i, d in enumerate(distances):
        out_ref[i] = term_at(w_ref, gt_ref, d)


def relay_message(at, terms_ref, f_ref, b_ref, sums_ref, fwd_ref, bwd_ref):
    width = terms_ref.shape[1] // YL
    sums = sums_ref[...]
    whole = len(f_ref.shape) == 3
    for i, (got, ref) in enumerate(((f_ref, fwd_ref), (b_ref, bwd_ref))):
        for y in range(YL):
            term = terms_ref[at + i, y * width : (y + 1) * width]
            if whole or y == i:
                source = got.at[y] if whole else got
                ref[y, :width] = (term.astype(F32) + source[:width].astype(F32)).astype(BF)
                ref[y, width:] = pack(unpack(source[width:]) + sums)
            else:
                ref[y, :width] = term
                ref[y, width:] = pack(sums)


def swap_message(at, terms_ref, f_ref, b_ref, sums_ref, mine_ref, other_ref):
    width = terms_ref.shape[1] // YL
    yl = yl_index()
    for ref, y in ((mine_ref, yl), (other_ref, 1 - yl)):
        term = terms_ref[at, pl.ds(pl.multiple_of(y * width, width), width)]
        ref[:width] = wide_sum(term, f_ref[y, :width], b_ref[y, :width]).astype(BF)
        ref[width:] = pack(unpack(f_ref[y, width:]) + unpack(b_ref[y, width:]) + sums_ref[...])


def finish_tokens(mine_ref, other_ref, tok_ref, gain_ref, stats_ref, out_ref):
    rows, width = tok_ref.shape
    cols = width * Z * YL
    grad = wide_sum(mine_ref[:width], other_ref[:width]).T
    sums = (unpack(mine_ref[width:]) + unpack(other_ref[width:])).T / cols
    stats = stats_ref[...].T
    inv = stats[:, 1:2]
    scaled = grad * gain_ref[lax.axis_index("mp")]
    unit = (tok_ref[...].astype(F32) - stats[:, 0:1]) * inv
    out_ref[...] = (inv * (scaled - sums[:, 0:1] - unit * sums[:, 1:2])).astype(BF)


def weight_terms(places, start, size, own_ref, sib_ref, gt_ref, gs_ref, *outs):
    x0, yh = x_index(), yh_index()
    left = jnp.concatenate([gt_ref[start : start + size], gs_ref[start : start + size]], 1)
    for i, (dx, h) in enumerate(places):
        h = yh if h is None else 1 - yh if h < 0 else h
        block = lax.rem(x0 + dx, X) * YH + h
        right = jnp.concatenate([own_ref[block], sib_ref[block]], 0)
        term = dot_nn(left, right).astype(BF)
        if len(outs) == 1:
            outs[0][i] = term
        else:
            outs[i][...] = term


def wide_sum(*parts):
    total = parts[0].astype(F32)
    for part in parts[1:]:
        total = total + part.astype(F32)
    return total


def main_message(near_ref, f_ref, b_ref, fwd_ref, bwd_ref):
    fwd_ref[0] = wide_sum(near_ref[0], f_ref[...]).astype(BF)
    fwd_ref[1] = near_ref[1]
    bwd_ref[0] = near_ref[2]
    bwd_ref[1] = wide_sum(near_ref[3], b_ref[...]).astype(BF)


def main_swap(near_ref, f_ref, b_ref, mine_ref, other_ref):
    yh = yh_index()
    other = 1 - yh
    mine_ref[...] = wide_sum(near_ref[4 + yh], f_ref[yh], b_ref[yh])
    other_ref[...] = wide_sum(near_ref[4 + other], f_ref[other], b_ref[other]).astype(BF)


def rest_first(own_ref, got_ref, fwd_ref, bwd_ref):
    half = fwd_ref.shape[0]
    fwd_ref[...] = wide_sum(own_ref[0, :half], got_ref[0, :half]).astype(BF)
    bwd_ref[...] = wide_sum(own_ref[0, half:], got_ref[0, half:]).astype(BF)


def rest_second(own_ref, got_ref, f_ref, b_ref, fwd_ref, bwd_ref):
    half = f_ref.shape[0]
    fwd_ref[:half] = wide_sum(own_ref[1, :half], got_ref[1, :half], f_ref[...]).astype(BF)
    fwd_ref[half:] = wide_sum(own_ref[1, half:], got_ref[1, half:]).astype(BF)
    bwd_ref[:half] = wide_sum(own_ref[2, :half], got_ref[2, :half]).astype(BF)
    bwd_ref[half:] = wide_sum(own_ref[2, half:], got_ref[2, half:], b_ref[...]).astype(BF)


def finish_weight(mine_ref, got_ref, own_ref, other_ref, f_ref, b_ref, out_ref):
    main = mine_ref.shape[0]
    out_ref[:, :main] = wide_sum(mine_ref[...], got_ref[...]).T
    out_ref[:, main:] = wide_sum(own_ref[3], other_ref[3], f_ref[...], b_ref[...]).T


def local(tokens, ln_gain, w_qkv, q_gain, k_gain, d_out):
    rows, width = tokens.shape
    heads, n3 = w_qkv.shape[1:]
    n = heads * n3
    hd = n3 // 3
    main = n // 2
    rest = n - main
    gains = ln_gain.astype(F32).reshape(Z * YL, 1, width)
    head_gains = jnp.stack([q_gain, k_gain]).astype(F32)

    with jax.named_scope("gather"):
        blocks, w, tokens = gather_tokens(tokens, w_qkv, gains, head_gains)
    blocks_shape = ((Z, rows, width), BF)
    eight = ((8, rows), F32)
    shape = [((rows, n), F32), ((16, n), F32), blocks_shape, blocks_shape, eight]
    qkv, wg, own, for_sib, stats = call(project, shape, *blocks, gains, w, limit=12)
    with jax.named_scope("core_rows"):
        sib = core_swap(for_sib)
    half = ((width + EXTRA, rows), BF)
    full = ((YL, width + EXTRA, rows), BF)
    shape = [((rows, heads * hd), BF, None), ((n, rows), BF), eight, half, half]
    kernel = functools.partial(attend, heads, hd)
    attn_out, gt, sums, to_fwd, to_bwd = call(
        kernel, shape, qkv, wg, head_gains, d_out, w, limit=8
    )
    with jax.named_scope("core_grads"):
        gs = core_swap(gt)
    with jax.named_scope("z_relay1"):
        fwd, bwd = z_step(to_fwd, 1), z_step(to_bwd, -1)

    def terms_at(distances, *deps):
        kernel = functools.partial(token_terms, distances)
        shape = [((len(distances), width * YL, rows), BF)]
        return call(kernel, shape, gt, w, deps=deps)[0]

    def weight(places, start, size, *deps, apart=False):
        kernel = functools.partial(weight_terms, places, start, size)
        shape = [((size, width), BF)] * len(places)
        if not apart:
            shape = [((len(places), size, width), BF)]
        outs = call(kernel, shape, own, sib, gt, gs, deps=deps)
        return outs if apart else outs[0]

    def relay(terms, at, fwd, bwd, *deps):
        kernel = functools.partial(relay_message, at)
        to_fwd, to_bwd = call(kernel, [full] * 2, terms, fwd, bwd, sums, deps=deps)
        return to_fwd, z_step(to_fwd, 1), z_step(to_bwd, -1)

    near_terms = terms_at((3, 5))
    far_fwd, far_bwd = weight(((2, 0), (2, 1)), 0, main, near_terms, apart=True)
    with jax.named_scope("x_main1"):
        w_fwd, w_bwd = x_step(far_fwd, 1), x_step(far_bwd, -1)
    with jax.named_scope("z_relay2"):
        sent, fwd, bwd = relay(near_terms, 0, fwd, bwd, far_fwd)
    r_other = weight(tuple((dx, -1) for dx in (2, 1, 3, 0)), main, rest, sent)
    with jax.named_scope("yh_rest"):
        r_got = yh_swap(r_other)
    places = tuple((dx, h) for dx in (1, 3, 0) for h in range(YH))
    w_near = weight(places, 0, main, r_other)
    terms = terms_at((2, 6, 1, 7, 0), w_near)
    with jax.named_scope("x_main2"):
        message = ((YH, main, width), BF)
        sent, to_bwd = call(main_message, [message] * 2, w_near, w_fwd, w_bwd, deps=[terms])
        w_fwd, w_bwd = x_step(sent, 1), x_step(to_bwd, -1)
    r_own = weight(tuple((dx, None) for dx in (2, 1, 3, 0)), main, rest, sent)
    with jax.named_scope("z_relay3"):
        sent, fwd, bwd = relay(terms, 0, fwd, bwd, r_own)
    with jax.named_scope("z_relay4"):
        sent, fwd, bwd = relay(terms, 2, fwd, bwd)
    with jax.named_scope("x_rest1"):
        shape = [((rest // 2, width), BF)] * 2
        to_fwd, to_bwd = call(rest_first, shape, r_own, r_got, deps=[sent])
        r_fwd, r_bwd = x_step(to_fwd, 1), x_step(to_bwd, -1)
    with jax.named_scope("yh_main"):
        shape = [((main, width), F32), ((main, width), BF)]
        mine, other = call(main_swap, shape, w_near, w_fwd, w_bwd, deps=[to_fwd])
        got = yh_swap(other)
    with jax.named_scope("x_rest2"):
        shape = [((rest, width), BF)] * 2
        to_fwd, to_bwd = call(rest_second, shape, r_own, r_got, r_fwd, r_bwd, deps=[other])
        r_fwd, r_bwd = x_step(to_fwd, 1), x_step(to_bwd, -1)
    with jax.named_scope("y_tokens"):
        kernel = functools.partial(swap_message, 4)
        to_mine, to_other = call(kernel, [half] * 2, terms, fwd, bwd, sums, deps=[to_fwd])
        got_y = yl_swap(to_other)
        shape = [((rows, width), BF, None)]
        grad_tokens = call(finish_tokens, shape, to_mine, got_y, tokens, gains, stats)[0]
    with jax.named_scope("weight_out"):
        shape = [((width, n), F32)]
        flat = call(finish_weight, shape, mine, got, r_own, r_got, r_fwd, r_bwd)[0]
    return attn_out, grad_tokens, flat.reshape(width, heads, n3)


def solution(mesh):
    in_specs = (P("dp", "mp"), P(), P(None, "mp", None), P(), P(), P("dp", "mp"))
    out_specs = (P("dp", "mp"), P("dp", "mp"), P("dp", "mp", None))
    return jax.shard_map(local, mesh=mesh, in_specs=in_specs, out_specs=out_specs, check_vma=False)
```

```python
import functools
import jax
import jax.numpy as jnp
from jax import lax
from jax.experimental import pallas as pl
from jax.experimental.pallas import tpu as pltpu
from jax.sharding import PartitionSpec as P

EPSILON = 1e-06
Z, YL, X, YH, CORES = 8, 2, 4, 2, 2
BF, F32 = jnp.bfloat16, jnp.float32
MIB = 1 << 20
GROUP = 16
EXTRA = 16
FAR = Z // 2
COST = pl.CostEstimate(flops=1024, bytes_accessed=1024, transcendentals=0)


def z_step(values, d):
    pairs = [(z * YL + y, ((z + d) % Z) * YL + y) for z in range(Z) for y in range(YL)]
    return lax.ppermute(values, "mp", pairs)


def yl_swap(values):
    return lax.ppermute(values, "mp", [(i, i ^ 1) for i in range(Z * YL)])


def x_step(values, d):
    n = YH * CORES
    pairs = [(x * n + r, ((x + d) % X) * n + r) for x in range(X) for r in range(n)]
    return lax.ppermute(values, "dp", pairs)


def yh_swap(values):
    return lax.ppermute(values, "dp", [(i, i ^ 2) for i in range(X * YH * CORES)])


def core_swap(values):
    return lax.ppermute(values, "dp", [(i, i ^ 1) for i in range(X * YH * CORES)])


def z_index():
    return lax.axis_index("mp") // YL


def yl_index():
    return lax.rem(lax.axis_index("mp"), YL)


def x_index():
    return lax.axis_index("dp") // (YH * CORES)


def yh_index():
    return lax.rem(lax.axis_index("dp") // CORES, YH)


def core_index():
    return lax.rem(lax.axis_index("dp"), CORES)


def held(shape, dtype):
    return pltpu.VMEM(shape, dtype)


def call(kernel, out_shape, *args, deps=(), hbm=(), limit=6, scratch=()):
    vmem, anywhere = pl.BlockSpec(memory_space=pltpu.VMEM), pl.BlockSpec(memory_space=pl.ANY)
    specs = [anywhere if i in hbm else vmem for i in range(len(args))]
    count = len(args)
    name = getattr(kernel, "func", kernel).__name__

    def body(*refs):
        kernel(*refs[:count], *refs[count + len(deps) :])

    return pl.pallas_call(
        body,
        in_specs=specs + [anywhere] * len(deps),
        out_specs=[vmem] * len(out_shape),
        out_shape=[(jax.ShapeDtypeStruct if o[2:] else held)(o[0], o[1]) for o in out_shape],
        scratch_shapes=list(scratch),
        compiler_params=pltpu.CompilerParams(vmem_limit_bytes=limit * MIB),
        cost_estimate=COST,
        name=name,
    )(*args, *deps)


def tie(values, dep, limit):
    anywhere = pl.BlockSpec(memory_space=pl.ANY)
    count = len(values)
    return pl.pallas_call(
        lambda *refs: None,
        in_specs=[anywhere] * (count + 1),
        out_specs=[anywhere] * count,
        out_shape=[jax.ShapeDtypeStruct(v.shape, v.dtype) for v in values],
        input_output_aliases={i: i for i in range(count)},
        compiler_params=pltpu.CompilerParams(vmem_limit_bytes=limit * MIB),
        cost_estimate=COST,
        name="tie",
    )(*values, dep)


def hold(ref, out_ref):
    out_ref[...] = ref[...]


def pair(own_ref, other_ref, out_ref):
    out_ref[0] = own_ref[...]
    out_ref[1] = other_ref[...]


def load(source, out_ref, sems):
    groups = out_ref.shape[0] // Z
    copies = []
    for i in range(Z):
        part = pl.ds(i * groups, groups)
        copies.append(pltpu.make_async_copy(source.at[part], out_ref.at[part], sems.at[i]))
        copies[-1].start()
    for copy in copies:
        copy.wait()


def gather_tokens(tokens, w_qkv, *early):
    other = yl_swap(tokens)
    tokens = call(hold, [(tokens.shape, BF)], tokens, deps=early)[0]
    blocks = {0: call(pair, [((YL, *tokens.shape), BF)], tokens, other)[0]}
    w = w_qkv.reshape(-1, GROUP, *w_qkv.shape[1:]).swapaxes(1, 2)
    for s in range(1, FAR):
        blocks[Z - s] = z_step(blocks[(Z - s + 1) % Z], 1)
        blocks[s] = z_step(blocks[s - 1], -1)
        if s == 1:
            blocks[Z - s], blocks[s] = tie([blocks[Z - s], blocks[s]], w, 46)
        if s == 2:
            shape, sems = [(w.shape, BF)], [pltpu.SemaphoreType.DMA((Z,))]
            deps = [blocks[1]]
            w = call(load, shape, w, deps=deps, hbm=[0], limit=46, scratch=sems)[0]
            blocks[Z - s], blocks[s] = tie([blocks[Z - s], blocks[s]], w, 1)
    blocks[FAR] = z_step(blocks[FAR + 1], 1)
    return [blocks[d] for d in range(Z)], w, tokens


def joined(w_ref):
    heads, columns = w_ref.shape[1], w_ref.shape[3]
    return jnp.concatenate([w_ref[:, h].reshape(-1, columns) for h in range(heads)], 1)


def project(*refs):
    blocks = refs[:Z]
    gain_ref, w_ref, qkv_ref, wg_ref, own_ref, sib_ref, stats_ref = refs[Z:]
    z0, yl, core = z_index(), yl_index(), core_index()
    rows, width = blocks[0].shape[1:]
    cols = width * YL * Z

    acc = jnp.zeros((rows, width), F32)
    acc2 = jnp.zeros((rows, width), F32)
    for d in range(Z):
        for r in range(YL):
            v = blocks[d][r].astype(F32)
            acc = acc + v
            acc2 = acc2 + v * v
    mean = jnp.sum(acc, 1, keepdims=True) / cols
    square = jnp.sum(acc2, 1, keepdims=True) / cols
    inv = lax.rsqrt(square - mean * mean + EPSILON)
    lane = lax.broadcasted_iota(jnp.int32, (rows, 128), 1)
    stats_ref[...] = jnp.where(lane == 0, mean, jnp.where(lane == 1, inv, 0.0)).T[:8]
    qkv_ref[...] = jnp.zeros_like(qkv_ref)
    wg_ref[...] = jnp.zeros_like(wg_ref)
    groups = w_ref.shape[0] // (Z * YL)

    for d in range(Z):
        zd = lax.rem(z0 + d, Z)
        ys = (yl, 1 - yl)
        gains = [gain_ref[zd * YL + y] for y in ys]
        parts = [
            ((blocks[d][r].astype(F32) - mean) * inv * g).astype(BF) for r, g in enumerate(gains)
        ]
        own_ref[zd] = jnp.where(core == yl, parts[0], parts[1])
        sib_ref[zd] = jnp.where(core == yl, parts[1], parts[0])
        extra = jnp.broadcast_to(jnp.concatenate(gains, 1), (16, width * YL)).astype(BF)
        left = jnp.concatenate([jnp.concatenate(parts, 1), extra], 0)
        firsts = [(zd * YL + y) * groups for y in ys]
        right = jnp.concatenate([joined(w_ref.at[pl.ds(f, groups)]) for f in firsts], 0)
        product = jnp.dot(left, right, preferred_element_type=F32)
        qkv_ref[...] += product[:rows]
        wg_ref[...] += product[rows:]


def dot_nt(a, b):
    return lax.dot_general(a, b, (((1,), (1,)), ((), ())), preferred_element_type=F32)


def dot_tn(a, b):
    return lax.dot_general(a, b, (((0,), (0,)), ((), ())), preferred_element_type=F32)


def dot_nn(a, b):
    return jnp.dot(a, b, preferred_element_type=F32)


def head_norm(values):
    centred = values - jnp.mean(values, -1, keepdims=True)
    inv = lax.rsqrt(jnp.mean(centred * centred, -1, keepdims=True) + EPSILON)
    return centred * inv, inv


def norm_back(grad, gain, unit, inv):
    scaled = grad * gain
    return inv * (
        scaled
        - jnp.mean(scaled, -1, keepdims=True)
        - unit * jnp.mean(scaled * unit, -1, keepdims=True)
    )


def pack(sums):
    high = sums.astype(BF).astype(F32)
    return jnp.concatenate([high, sums - high], 0).astype(BF)


def unpack(extra):
    wide = extra.astype(F32)
    half = wide.shape[0] // 2
    return wide[:half] + wide[half:]


def attend(heads, hd, qkv_ref, wg_ref, gains_ref, do_ref, w_ref, *outs):
    out_ref, gt_ref, sums_ref, fwd_ref, bwd_ref = outs
    scale = hd ** (-0.5)
    q_gain, k_gain = gains_ref[0:1], gains_ref[1:2]
    rows = qkv_ref.shape[0]
    acc_sum = jnp.zeros((rows, hd), F32)
    acc_cross = jnp.zeros((rows, hd), F32)
    for h in range(heads):
        base = h * 3 * hd
        q, k, v = (qkv_ref[:, base + i * hd : base + (i + 1) * hd] for i in range(3))
        q_unit, q_inv = head_norm(q)
        k_unit, k_inv = head_norm(k)
        q_half = (q_unit * q_gain).astype(BF)
        k_half = (k_unit * k_gain).astype(BF)
        v_half = v.astype(BF)
        d_out = do_ref[:, h * hd : (h + 1) * hd]
        exps = jnp.exp(dot_nt(q_half, k_half) * scale)
        probs = exps / jnp.sum(exps, -1, keepdims=True)
        probs_half = probs.astype(BF)
        out_ref[:, h * hd : (h + 1) * hd] = dot_nn(probs_half, v_half).astype(BF)
        grad_probs = dot_nt(d_out, v_half)
        grad_value = dot_tn(probs_half, d_out)
        inner = jnp.sum(probs * grad_probs, -1, keepdims=True)
        grad_scores = (probs * (grad_probs - inner) * scale).astype(BF)
        grad_q = norm_back(dot_nn(grad_scores, k_half), q_gain, q_unit, q_inv)
        grad_k = norm_back(dot_tn(grad_scores, q_half), k_gain, k_unit, k_inv)
        for i, (part, source) in enumerate(((grad_q, q), (grad_k, k), (grad_value, v))):
            cols = slice(base + i * hd, base + (i + 1) * hd)
            half = part.astype(BF)
            gt_ref[cols, :] = half.T
            wide = half.astype(F32)
            acc_sum = acc_sum + wide * wg_ref[0:1, cols]
            acc_cross = acc_cross + wide * source
    sums = jnp.sum(acc_sum, -1, keepdims=True)
    cross = jnp.sum(acc_cross, -1, keepdims=True)
    lane = lax.broadcasted_iota(jnp.int32, (rows, hd), 1)
    both = jnp.where(lane == 0, sums, jnp.where(lane == 1, cross, 0.0))
    sums = both.T[:8]
    sums_ref[...] = sums
    extra = pack(sums)
    width = fwd_ref.shape[0] - extra.shape[0]
    term = term_at(w_ref, gt_ref, FAR)
    for ref, part in ((fwd_ref, term[:width]), (bwd_ref, term[width:])):
        ref[:width] = part
        ref[width:] = extra


def term_at(w_ref, gt_ref, d):
    groups = w_ref.shape[0] // Z
    start = lax.rem(z_index() + d, Z) * groups
    return dot_nn(joined(w_ref.at[pl.ds(start, groups)]), gt_ref[...]).astype(BF)


def token_terms(distances, gt_ref, w_ref, out_ref):
    for i, d in enumerate(distances):
        out_ref[i] = term_at(w_ref, gt_ref, d)


def relay_message(at, terms_ref, f_ref, b_ref, sums_ref, fwd_ref, bwd_ref):
    width = terms_ref.shape[1] // YL
    sums = sums_ref[...]
    whole = len(f_ref.shape) == 3
    for i, (got, ref) in enumerate(((f_ref, fwd_ref), (b_ref, bwd_ref))):
        for y in range(YL):
            term = terms_ref[at + i, y * width : (y + 1) * width]
            if whole or y == i:
                source = got.at[y] if whole else got
                ref[y, :width] = (term.astype(F32) + source[:width].astype(F32)).astype(BF)
                ref[y, width:] = pack(unpack(source[width:]) + sums)
            else:
                ref[y, :width] = term
                ref[y, width:] = pack(sums)


def swap_message(at, terms_ref, f_ref, b_ref, sums_ref, mine_ref, other_ref):
    width = terms_ref.shape[1] // YL
    yl = yl_index()
    for ref, y in ((mine_ref, yl), (other_ref, 1 - yl)):
        term = terms_ref[at, pl.ds(pl.multiple_of(y * width, width), width)]
        ref[:width] = wide_sum(term, f_ref[y, :width], b_ref[y, :width]).astype(BF)
        ref[width:] = pack(unpack(f_ref[y, width:]) + unpack(b_ref[y, width:]) + sums_ref[...])


def finish_tokens(mine_ref, other_ref, tok_ref, gain_ref, stats_ref, out_ref):
    rows, width = tok_ref.shape
    cols = width * Z * YL
    grad = wide_sum(mine_ref[:width], other_ref[:width]).T
    sums = (unpack(mine_ref[width:]) + unpack(other_ref[width:])).T / cols
    stats = stats_ref[...].T
    inv = stats[:, 1:2]
    scaled = grad * gain_ref[lax.axis_index("mp")]
    unit = (tok_ref[...].astype(F32) - stats[:, 0:1]) * inv
    out_ref[...] = (inv * (scaled - sums[:, 0:1] - unit * sums[:, 1:2])).astype(BF)


def weight_terms(places, start, size, own_ref, sib_ref, gt_ref, gs_ref, outs):
    x0, yh = x_index(), yh_index()
    left = jnp.concatenate([gt_ref[start : start + size], gs_ref[start : start + size]], 1)
    for (dx, h), out in zip(places, outs):
        h = yh if h is None else 1 - yh if h < 0 else h
        block = lax.rem(x0 + dx, X) * YH + h
        right = jnp.concatenate([own_ref[block], sib_ref[block]], 0)
        out[...] = dot_nn(left, right).astype(BF)


def first_terms(own_ref, sib_ref, gt_ref, gs_ref, w_ref, fwd_ref, bwd_ref, other_ref, terms_ref):
    main = fwd_ref.shape[0]
    arrays = own_ref, sib_ref, gt_ref, gs_ref
    weight_terms(((2, 0), (2, 1)), 0, main, *arrays, (fwd_ref, bwd_ref))
    others = [other_ref.at[i] for i in range(X)]
    weight_terms([(dx, -1) for dx in (2, 1, 3, 0)], main, other_ref.shape[1], *arrays, others)
    token_terms((3, 5), gt_ref, w_ref, terms_ref)


def later_terms(own_ref, sib_ref, gt_ref, gs_ref, w_ref, near_ref, same_ref, terms_ref):
    main = near_ref.shape[1]
    arrays = own_ref, sib_ref, gt_ref, gs_ref
    places = [(dx, h) for dx in (1, 3, 0) for h in range(YH)]
    weight_terms(places, 0, main, *arrays, [near_ref.at[i] for i in range(len(places))])
    sames = [same_ref.at[i] for i in range(X)]
    weight_terms([(dx, None) for dx in (2, 1, 3, 0)], main, same_ref.shape[1], *arrays, sames)
    token_terms((2, 6, 1, 7, 0), gt_ref, w_ref, terms_ref)


def wide_sum(*parts):
    total = parts[0].astype(F32)
    for part in parts[1:]:
        total = total + part.astype(F32)
    return total


def main_message(near_ref, f_ref, b_ref, fwd_ref, bwd_ref):
    fwd_ref[0] = wide_sum(near_ref[0], f_ref[...]).astype(BF)
    fwd_ref[1] = near_ref[1]
    bwd_ref[0] = near_ref[2]
    bwd_ref[1] = wide_sum(near_ref[3], b_ref[...]).astype(BF)


def main_swap(near_ref, f_ref, b_ref, mine_ref, other_ref):
    yh = yh_index()
    other = 1 - yh
    mine_ref[...] = wide_sum(near_ref[4 + yh], f_ref[yh], b_ref[yh])
    other_ref[...] = wide_sum(near_ref[4 + other], f_ref[other], b_ref[other]).astype(BF)


def rest_first(own_ref, got_ref, fwd_ref, bwd_ref):
    half = fwd_ref.shape[0]
    fwd_ref[...] = wide_sum(own_ref[0, :half], got_ref[0, :half]).astype(BF)
    bwd_ref[...] = wide_sum(own_ref[0, half:], got_ref[0, half:]).astype(BF)


def rest_second(own_ref, got_ref, f_ref, b_ref, fwd_ref, bwd_ref):
    half = f_ref.shape[0]
    fwd_ref[:half] = wide_sum(own_ref[1, :half], got_ref[1, :half], f_ref[...]).astype(BF)
    fwd_ref[half:] = wide_sum(own_ref[1, half:], got_ref[1, half:]).astype(BF)
    bwd_ref[:half] = wide_sum(own_ref[2, :half], got_ref[2, :half]).astype(BF)
    bwd_ref[half:] = wide_sum(own_ref[2, half:], got_ref[2, half:], b_ref[...]).astype(BF)


def finish_weight(mine_ref, got_ref, own_ref, other_ref, f_ref, b_ref, out_ref):
    main, n3 = mine_ref.shape[0], out_ref.shape[2]
    parts = [
        wide_sum(mine_ref[...], got_ref[...]),
        wide_sum(own_ref[3], other_ref[3], f_ref[...], b_ref[...]),
    ]
    whole = jnp.concatenate(parts, 0)
    for h in range(out_ref.shape[1]):
        out_ref[:, h, :] = whole[h * n3 : (h + 1) * n3].T


def local(tokens, ln_gain, w_qkv, q_gain, k_gain, d_out):
    rows, width = tokens.shape
    heads, n3 = w_qkv.shape[1:]
    n = heads * n3
    hd = n3 // 3
    main = n // 2
    rest = n - main
    gains = ln_gain.astype(F32).reshape(Z * YL, 1, width)
    head_gains = jnp.stack([q_gain, k_gain]).astype(F32)

    with jax.named_scope("gather"):
        blocks, w, tokens = gather_tokens(tokens, w_qkv, gains, head_gains)
    blocks_shape = ((Z, rows, width), BF)
    eight = ((8, rows), F32)
    shape = [((rows, n), F32), ((16, n), F32), blocks_shape, blocks_shape, eight]
    qkv, wg, own, for_sib, stats = call(project, shape, *blocks, gains, w, limit=12)
    with jax.named_scope("core_rows"):
        sib = core_swap(for_sib)
    half = ((width + EXTRA, rows), BF)
    full = ((YL, width + EXTRA, rows), BF)
    shape = [((rows, heads * hd), BF, None), ((n, rows), BF), eight, half, half]
    kernel = functools.partial(attend, heads, hd)
    attn_out, gt, sums, to_fwd, to_bwd = call(
        kernel, shape, qkv, wg, head_gains, d_out, w, limit=8
    )
    with jax.named_scope("core_grads"):
        gs = core_swap(gt)
    with jax.named_scope("z_relay1"):
        fwd, bwd = z_step(to_fwd, 1), z_step(to_bwd, -1)

    def relay(terms, at, fwd, bwd, *deps):
        kernel = functools.partial(relay_message, at)
        to_fwd, to_bwd = call(kernel, [full] * 2, terms, fwd, bwd, sums, deps=deps)
        return to_fwd, z_step(to_fwd, 1), z_step(to_bwd, -1)

    one, wide = ((main, width), BF), width * YL
    shape = [one, one, ((X, rest, width), BF), ((2, wide, rows), BF)]
    far_fwd, far_bwd, r_other, near_terms = call(first_terms, shape, own, sib, gt, gs, w)
    with jax.named_scope("x_main1"):
        w_fwd, w_bwd = x_step(far_fwd, 1), x_step(far_bwd, -1)
    with jax.named_scope("yh_rest"):
        r_got = yh_swap(r_other)
    with jax.named_scope("z_relay2"):
        sent, fwd, bwd = relay(near_terms, 0, fwd, bwd)
    shape = [((6, main, width), BF), ((X, rest, width), BF), ((5, wide, rows), BF)]
    w_near, r_own, terms = call(later_terms, shape, own, sib, gt, gs, w, deps=[sent])
    with jax.named_scope("x_main2"):
        message = ((YH, main, width), BF)
        to_fwd, to_bwd = call(main_message, [message] * 2, w_near, w_fwd, w_bwd)
        w_fwd, w_bwd = x_step(to_fwd, 1), x_step(to_bwd, -1)
    with jax.named_scope("z_relay3"):
        sent, fwd, bwd = relay(terms, 0, fwd, bwd, to_fwd)
    with jax.named_scope("z_relay4"):
        sent, fwd, bwd = relay(terms, 2, fwd, bwd)
    with jax.named_scope("x_rest1"):
        shape = [((rest // 2, width), BF)] * 2
        to_fwd, to_bwd = call(rest_first, shape, r_own, r_got, deps=[sent])
        r_fwd, r_bwd = x_step(to_fwd, 1), x_step(to_bwd, -1)
    with jax.named_scope("yh_main"):
        shape = [((main, width), F32), ((main, width), BF)]
        mine, other = call(main_swap, shape, w_near, w_fwd, w_bwd, deps=[to_fwd])
        got = yh_swap(other)
    with jax.named_scope("x_rest2"):
        shape = [((rest, width), BF)] * 2
        to_fwd, to_bwd = call(rest_second, shape, r_own, r_got, r_fwd, r_bwd, deps=[other])
        r_fwd, r_bwd = x_step(to_fwd, 1), x_step(to_bwd, -1)
    with jax.named_scope("y_tokens"):
        kernel = functools.partial(swap_message, 4)
        to_mine, to_other = call(kernel, [half] * 2, terms, fwd, bwd, sums, deps=[to_fwd])
        got_y = yl_swap(to_other)
        shape = [((rows, width), BF, None)]
        grad_tokens = call(finish_tokens, shape, to_mine, got_y, tokens, gains, stats)[0]
    with jax.named_scope("weight_out"):
        shape = [((width, heads, n3), F32, None)]
        grad_weight = call(finish_weight, shape, mine, got, r_own, r_got, r_fwd, r_bwd)[0]
    return attn_out, grad_tokens, grad_weight


def solution(mesh):
    in_specs = (P("dp", "mp"), P(), P(None, "mp", None), P(), P(), P("dp", "mp"))
    out_specs = (P("dp", "mp"), P("dp", "mp"), P("dp", "mp", None))
    return jax.shard_map(local, mesh=mesh, in_specs=in_specs, out_specs=out_specs, check_vma=False)
```

```python
import functools
import jax
import jax.numpy as jnp
from jax import lax
from jax.experimental import pallas as pl
from jax.experimental.pallas import tpu as pltpu
from jax.sharding import PartitionSpec as P

EPSILON = 1e-06
Z, YL, X, YH, CORES = 8, 2, 4, 2, 2
BF, F32 = jnp.bfloat16, jnp.float32
MIB = 1 << 20
GROUP = 16
EXTRA = 16
FAR = Z // 2
COST = pl.CostEstimate(flops=1024, bytes_accessed=1024, transcendentals=0)


def z_step(values, d):
    pairs = [(z * YL + y, ((z + d) % Z) * YL + y) for z in range(Z) for y in range(YL)]
    return lax.ppermute(values, "mp", pairs)


def yl_swap(values):
    return lax.ppermute(values, "mp", [(i, i ^ 1) for i in range(Z * YL)])


def x_step(values, d):
    n = YH * CORES
    pairs = [(x * n + r, ((x + d) % X) * n + r) for x in range(X) for r in range(n)]
    return lax.ppermute(values, "dp", pairs)


def yh_swap(values):
    return lax.ppermute(values, "dp", [(i, i ^ 2) for i in range(X * YH * CORES)])


def core_swap(values):
    return lax.ppermute(values, "dp", [(i, i ^ 1) for i in range(X * YH * CORES)])


def z_index():
    return lax.axis_index("mp") // YL


def yl_index():
    return lax.rem(lax.axis_index("mp"), YL)


def x_index():
    return lax.axis_index("dp") // (YH * CORES)


def yh_index():
    return lax.rem(lax.axis_index("dp") // CORES, YH)


def core_index():
    return lax.rem(lax.axis_index("dp"), CORES)


def held(shape, dtype):
    return pltpu.VMEM(shape, dtype)


def call(kernel, out_shape, *args, deps=(), hbm=(), limit=6, scratch=()):
    vmem, anywhere = pl.BlockSpec(memory_space=pltpu.VMEM), pl.BlockSpec(memory_space=pl.ANY)
    specs = [anywhere if i in hbm else vmem for i in range(len(args))]
    count = len(args)
    name = getattr(kernel, "func", kernel).__name__

    def body(*refs):
        kernel(*refs[:count], *refs[count + len(deps) :])

    return pl.pallas_call(
        body,
        in_specs=specs + [anywhere] * len(deps),
        out_specs=[vmem] * len(out_shape),
        out_shape=[(jax.ShapeDtypeStruct if o[2:] else held)(o[0], o[1]) for o in out_shape],
        scratch_shapes=list(scratch),
        compiler_params=pltpu.CompilerParams(vmem_limit_bytes=limit * MIB),
        cost_estimate=COST,
        name=name,
    )(*args, *deps)


def tie(values, dep, limit):
    anywhere = pl.BlockSpec(memory_space=pl.ANY)
    count = len(values)
    return pl.pallas_call(
        lambda *refs: None,
        in_specs=[anywhere] * (count + 1),
        out_specs=[anywhere] * count,
        out_shape=[jax.ShapeDtypeStruct(v.shape, v.dtype) for v in values],
        input_output_aliases={i: i for i in range(count)},
        compiler_params=pltpu.CompilerParams(vmem_limit_bytes=limit * MIB),
        cost_estimate=COST,
        name="tie",
    )(*values, dep)


def hold(ref, out_ref):
    out_ref[...] = ref[...]


def pair(*refs):
    count = len(refs) // 3
    for i, out_ref in enumerate(refs[2 * count :]):
        out_ref[0] = refs[2 * i][...]
        out_ref[1] = refs[2 * i + 1][...]


def load(source, out_ref, sems):
    groups = out_ref.shape[0] // Z
    copies = []
    for i in range(Z):
        part = pl.ds(i * groups, groups)
        copies.append(pltpu.make_async_copy(source.at[part], out_ref.at[part], sems.at[i]))
        copies[-1].start()
    for copy in copies:
        copy.wait()


def gather_tokens(tokens, w_qkv, *early):
    other = yl_swap(tokens)
    own_up, own_down = z_step(tokens, 1), z_step(tokens, -1)
    tokens = call(hold, [(tokens.shape, BF)], tokens, deps=[*early, other])[0]
    other_up, other_down = z_step(other, 1), z_step(other, -1)
    blocks, shape = {}, ((YL, *tokens.shape), BF)
    blocks[Z - 1], blocks[1] = call(pair, [shape] * 2, own_up, other_up, own_down, other_down)
    blocks[0] = call(pair, [shape], tokens, other, deps=[blocks[1]])[0]
    w = w_qkv.reshape(-1, GROUP, *w_qkv.shape[1:]).swapaxes(1, 2)
    for s in range(2, FAR):
        blocks[Z - s] = z_step(blocks[Z - s + 1], 1)
        blocks[s] = z_step(blocks[s - 1], -1)
        if s == 2:
            blocks[Z - s], blocks[s] = tie([blocks[Z - s], blocks[s]], w, 46)
        if s == 3:
            out, sems = [(w.shape, BF)], [pltpu.SemaphoreType.DMA((Z,))]
            deps = [blocks[2]]
            w = call(load, out, w, deps=deps, hbm=[0], limit=46, scratch=sems)[0]
            blocks[s] = tie([blocks[s]], w, 1)[0]
    blocks[FAR] = z_step(blocks[FAR + 1], 1)
    return [blocks[d] for d in range(Z)], w, tokens


def joined(w_ref):
    heads, columns = w_ref.shape[1], w_ref.shape[3]
    return jnp.concatenate([w_ref[:, h].reshape(-1, columns) for h in range(heads)], 1)


def gains_at(gain_ref, d):
    z, yl = lax.rem(z_index() + d, Z), yl_index()
    return [gain_ref[z * YL + y] for y in (yl, 1 - yl)]


def w_at(w_ref, d):
    z, yl = lax.rem(z_index() + d, Z), yl_index()
    groups = w_ref.shape[0] // (Z * YL)
    firsts = [(z * YL + y) * groups for y in (yl, 1 - yl)]
    return jnp.concatenate([joined(w_ref.at[pl.ds(f, groups)]) for f in firsts], 0)


def row_sums(blocks):
    rows, width = blocks[0].shape[1:]
    acc = jnp.zeros((rows, width), F32)
    acc2 = jnp.zeros((rows, width), F32)
    for block in blocks:
        for r in range(YL):
            v = block[r].astype(F32)
            acc = acc + v
            acc2 = acc2 + v * v
    return jnp.sum(acc, 1, keepdims=True), jnp.sum(acc2, 1, keepdims=True)


def centred(block, shift, gains):
    return jnp.concatenate(
        [((block[r].astype(F32) - shift) * g).astype(BF) for r, g in enumerate(gains)], 1
    )


def project_near(*refs):
    *blocks, gain_ref, w_ref, part_ref, wg_ref, sums_ref = refs
    rows, width = blocks[0].shape[1:]
    total, square = row_sums(blocks)
    shift = total / (len(blocks) * YL * width)
    lane = lax.broadcasted_iota(jnp.int32, (rows, 128), 1)
    sums_ref[...] = jnp.where(lane == 0, total, jnp.where(lane == 1, square, shift))
    part_ref[...] = jnp.zeros_like(part_ref)
    wg_ref[...] = jnp.zeros_like(wg_ref)
    for d in range(Z):
        gains = gains_at(gain_ref, d)
        left = jnp.broadcast_to(jnp.concatenate(gains, 1), (16, width * YL)).astype(BF)
        if d == FAR:
            wg_ref[...] += dot_nn(left, w_at(w_ref, d))
            continue
        block = blocks[d if d < FAR else d - 1]
        left = jnp.concatenate([centred(block, shift, gains), left], 0)
        product = dot_nn(left, w_at(w_ref, d))
        part_ref[...] += product[:rows]
        wg_ref[...] += product[rows:]


def project(*refs):
    blocks = refs[:Z]
    gain_ref, w_ref, part_ref, wg_ref, sums_ref, qkv_ref, own_ref, sib_ref, stats_ref = refs[Z:]
    rows, width = blocks[0].shape[1:]
    cols = width * Z * YL
    total, square = row_sums([blocks[FAR]])
    mean = (total + sums_ref[:, 0:1]) / cols
    inv = lax.rsqrt((square + sums_ref[:, 1:2]) / cols - mean * mean + EPSILON)
    shift = sums_ref[:, 2:3]
    lane = lax.broadcasted_iota(jnp.int32, (rows, 128), 1)
    stats_ref[...] = jnp.where(lane == 0, mean, jnp.where(lane == 1, inv, 0.0)).T[:8]
    gains = gains_at(gain_ref, FAR)
    product = dot_nn(centred(blocks[FAR], shift, gains), w_at(w_ref, FAR))
    qkv_ref[...] = inv * (part_ref[...] + product - (mean - shift) * wg_ref[0:1])
    first = core_index() == yl_index()
    for d in range(Z):
        zd = lax.rem(z_index() + d, Z)
        parts = [
            ((blocks[d][r].astype(F32) - mean) * inv * g).astype(BF)
            for r, g in enumerate(gains_at(gain_ref, d))
        ]
        own_ref[zd] = jnp.where(first, parts[0], parts[1])
        sib_ref[zd] = jnp.where(first, parts[1], parts[0])


def dot_nt(a, b):
    return lax.dot_general(a, b, (((1,), (1,)), ((), ())), preferred_element_type=F32)


def dot_tn(a, b):
    return lax.dot_general(a, b, (((0,), (0,)), ((), ())), preferred_element_type=F32)


def dot_nn(a, b):
    return jnp.dot(a, b, preferred_element_type=F32)


def head_norm(values):
    centred = values - jnp.mean(values, -1, keepdims=True)
    inv = lax.rsqrt(jnp.mean(centred * centred, -1, keepdims=True) + EPSILON)
    return centred * inv, inv


def norm_back(grad, gain, unit, inv):
    scaled = grad * gain
    return inv * (
        scaled
        - jnp.mean(scaled, -1, keepdims=True)
        - unit * jnp.mean(scaled * unit, -1, keepdims=True)
    )


def pack(sums):
    high = sums.astype(BF).astype(F32)
    return jnp.concatenate([high, sums - high], 0).astype(BF)


def unpack(extra):
    wide = extra.astype(F32)
    half = wide.shape[0] // 2
    return wide[:half] + wide[half:]


def attend(heads, hd, qkv_ref, wg_ref, gains_ref, do_ref, w_ref, *outs):
    out_ref, gt_ref, sums_ref, fwd_ref, bwd_ref = outs
    scale = hd ** (-0.5)
    q_gain, k_gain = gains_ref[0:1], gains_ref[1:2]
    rows = qkv_ref.shape[0]
    acc_sum = jnp.zeros((rows, hd), F32)
    acc_cross = jnp.zeros((rows, hd), F32)
    for h in range(heads):
        base = h * 3 * hd
        q, k, v = (qkv_ref[:, base + i * hd : base + (i + 1) * hd] for i in range(3))
        q_unit, q_inv = head_norm(q)
        k_unit, k_inv = head_norm(k)
        q_half = (q_unit * q_gain).astype(BF)
        k_half = (k_unit * k_gain).astype(BF)
        v_half = v.astype(BF)
        d_out = do_ref[:, h * hd : (h + 1) * hd]
        exps = jnp.exp(dot_nt(q_half, k_half) * scale)
        probs = exps / jnp.sum(exps, -1, keepdims=True)
        probs_half = probs.astype(BF)
        out_ref[:, h * hd : (h + 1) * hd] = dot_nn(probs_half, v_half).astype(BF)
        grad_probs = dot_nt(d_out, v_half)
        grad_value = dot_tn(probs_half, d_out)
        inner = jnp.sum(probs * grad_probs, -1, keepdims=True)
        grad_scores = (probs * (grad_probs - inner) * scale).astype(BF)
        grad_q = norm_back(dot_nn(grad_scores, k_half), q_gain, q_unit, q_inv)
        grad_k = norm_back(dot_tn(grad_scores, q_half), k_gain, k_unit, k_inv)
        for i, (part, source) in enumerate(((grad_q, q), (grad_k, k), (grad_value, v))):
            cols = slice(base + i * hd, base + (i + 1) * hd)
            half = part.astype(BF)
            gt_ref[cols, :] = half.T
            wide = half.astype(F32)
            acc_sum = acc_sum + wide * wg_ref[0:1, cols]
            acc_cross = acc_cross + wide * source
    sums = jnp.sum(acc_sum, -1, keepdims=True)
    cross = jnp.sum(acc_cross, -1, keepdims=True)
    lane = lax.broadcasted_iota(jnp.int32, (rows, hd), 1)
    both = jnp.where(lane == 0, sums, jnp.where(lane == 1, cross, 0.0))
    sums = both.T[:8]
    sums_ref[...] = sums
    extra = pack(sums)
    width = fwd_ref.shape[0] - extra.shape[0]
    term = term_at(w_ref, gt_ref, FAR)
    for ref, part in ((fwd_ref, term[:width]), (bwd_ref, term[width:])):
        ref[:width] = part
        ref[width:] = extra


def term_at(w_ref, gt_ref, d):
    groups = w_ref.shape[0] // Z
    start = lax.rem(z_index() + d, Z) * groups
    return dot_nn(joined(w_ref.at[pl.ds(start, groups)]), gt_ref[...]).astype(BF)


def token_terms(distances, gt_ref, w_ref, out_ref):
    for i, d in enumerate(distances):
        out_ref[i] = term_at(w_ref, gt_ref, d)


def relay_message(at, terms_ref, f_ref, b_ref, sums_ref, fwd_ref, bwd_ref):
    width = terms_ref.shape[1] // YL
    sums = sums_ref[...]
    whole = len(f_ref.shape) == 3
    for i, (got, ref) in enumerate(((f_ref, fwd_ref), (b_ref, bwd_ref))):
        for y in range(YL):
            term = terms_ref[at + i, y * width : (y + 1) * width]
            if whole or y == i:
                source = got.at[y] if whole else got
                ref[y, :width] = (term.astype(F32) + source[:width].astype(F32)).astype(BF)
                ref[y, width:] = pack(unpack(source[width:]) + sums)
            else:
                ref[y, :width] = term
                ref[y, width:] = pack(sums)


def swap_message(at, terms_ref, f_ref, b_ref, sums_ref, mine_ref, other_ref):
    width = terms_ref.shape[1] // YL
    yl = yl_index()
    for ref, y in ((mine_ref, yl), (other_ref, 1 - yl)):
        term = terms_ref[at, pl.ds(pl.multiple_of(y * width, width), width)]
        ref[:width] = wide_sum(term, f_ref[y, :width], b_ref[y, :width]).astype(BF)
        ref[width:] = pack(unpack(f_ref[y, width:]) + unpack(b_ref[y, width:]) + sums_ref[...])


def finish_tokens(mine_ref, other_ref, tok_ref, gain_ref, stats_ref, out_ref):
    rows, width = tok_ref.shape
    cols = width * Z * YL
    grad = wide_sum(mine_ref[:width], other_ref[:width]).T
    sums = (unpack(mine_ref[width:]) + unpack(other_ref[width:])).T / cols
    stats = stats_ref[...].T
    inv = stats[:, 1:2]
    scaled = grad * gain_ref[lax.axis_index("mp")]
    unit = (tok_ref[...].astype(F32) - stats[:, 0:1]) * inv
    out_ref[...] = (inv * (scaled - sums[:, 0:1] - unit * sums[:, 1:2])).astype(BF)


def weight_terms(places, start, size, own_ref, sib_ref, gt_ref, gs_ref, outs):
    x0, yh = x_index(), yh_index()
    left = jnp.concatenate([gt_ref[start : start + size], gs_ref[start : start + size]], 1)
    for (dx, h), out in zip(places, outs):
        h = yh if h is None else 1 - yh if h < 0 else h
        block = lax.rem(x0 + dx, X) * YH + h
        right = jnp.concatenate([own_ref[block], sib_ref[block]], 0)
        out[...] = dot_nn(left, right).astype(BF)


def first_terms(own_ref, sib_ref, gt_ref, gs_ref, w_ref, fwd_ref, bwd_ref, other_ref, terms_ref):
    main = fwd_ref.shape[0]
    arrays = own_ref, sib_ref, gt_ref, gs_ref
    weight_terms(((2, 0), (2, 1)), 0, main, *arrays, (fwd_ref, bwd_ref))
    others = [other_ref.at[i] for i in range(X)]
    weight_terms([(dx, -1) for dx in (2, 1, 3, 0)], main, other_ref.shape[1], *arrays, others)
    token_terms((3, 5), gt_ref, w_ref, terms_ref)


def later_terms(own_ref, sib_ref, gt_ref, gs_ref, w_ref, near_ref, same_ref, terms_ref):
    main = near_ref.shape[1]
    arrays = own_ref, sib_ref, gt_ref, gs_ref
    places = [(dx, h) for dx in (1, 3, 0) for h in range(YH)]
    weight_terms(places, 0, main, *arrays, [near_ref.at[i] for i in range(len(places))])
    sames = [same_ref.at[i] for i in range(X)]
    weight_terms([(dx, None) for dx in (2, 1, 3, 0)], main, same_ref.shape[1], *arrays, sames)
    token_terms((2, 6, 1, 7, 0), gt_ref, w_ref, terms_ref)


def wide_sum(*parts):
    total = parts[0].astype(F32)
    for part in parts[1:]:
        total = total + part.astype(F32)
    return total


def main_message(near_ref, f_ref, b_ref, fwd_ref, bwd_ref):
    fwd_ref[0] = wide_sum(near_ref[0], f_ref[...]).astype(BF)
    fwd_ref[1] = near_ref[1]
    bwd_ref[0] = near_ref[2]
    bwd_ref[1] = wide_sum(near_ref[3], b_ref[...]).astype(BF)


def main_swap(near_ref, f_ref, b_ref, mine_ref, other_ref):
    yh = yh_index()
    other = 1 - yh
    mine_ref[...] = wide_sum(near_ref[4 + yh], f_ref[yh], b_ref[yh])
    other_ref[...] = wide_sum(near_ref[4 + other], f_ref[other], b_ref[other]).astype(BF)


def rest_first(own_ref, got_ref, fwd_ref, bwd_ref):
    half = fwd_ref.shape[0]
    fwd_ref[...] = wide_sum(own_ref[0, :half], got_ref[0, :half]).astype(BF)
    bwd_ref[...] = wide_sum(own_ref[0, half:], got_ref[0, half:]).astype(BF)


def rest_second(own_ref, got_ref, f_ref, b_ref, fwd_ref, bwd_ref):
    half = f_ref.shape[0]
    fwd_ref[:half] = wide_sum(own_ref[1, :half], got_ref[1, :half], f_ref[...]).astype(BF)
    fwd_ref[half:] = wide_sum(own_ref[1, half:], got_ref[1, half:]).astype(BF)
    bwd_ref[:half] = wide_sum(own_ref[2, :half], got_ref[2, :half]).astype(BF)
    bwd_ref[half:] = wide_sum(own_ref[2, half:], got_ref[2, half:], b_ref[...]).astype(BF)


def finish_weight(mine_ref, got_ref, own_ref, other_ref, f_ref, b_ref, out_ref, done_ref):
    done_ref[...] = jnp.zeros_like(done_ref)
    main, n3 = mine_ref.shape[0], out_ref.shape[2]
    parts = [
        wide_sum(mine_ref[...], got_ref[...]),
        wide_sum(own_ref[3], other_ref[3], f_ref[...], b_ref[...]),
    ]
    whole = jnp.concatenate(parts, 0)
    for h in range(out_ref.shape[1]):
        out_ref[:, h, :] = whole[h * n3 : (h + 1) * n3].T


def local(tokens, ln_gain, w_qkv, q_gain, k_gain, d_out):
    rows, width = tokens.shape
    heads, n3 = w_qkv.shape[1:]
    n = heads * n3
    hd = n3 // 3
    main = n // 2
    rest = n - main
    gains = ln_gain.astype(F32).reshape(Z * YL, 1, width)
    head_gains = jnp.stack([q_gain, k_gain]).astype(F32)

    with jax.named_scope("gather"):
        blocks, w, tokens = gather_tokens(tokens, w_qkv, gains, head_gains)
    blocks_shape = ((Z, rows, width), BF)
    eight = ((8, rows), F32)
    qkv_shape = ((rows, n), F32)
    near = blocks[:FAR] + blocks[FAR + 1 :]
    shape = [qkv_shape, ((16, n), F32), ((rows, 128), F32)]
    part, wg, row_part = call(project_near, shape, *near, gains, w, limit=12)
    shape = [qkv_shape, blocks_shape, blocks_shape, eight]
    operands = [*blocks, gains, w, part, wg, row_part]
    qkv, own, for_sib, stats = call(project, shape, *operands, limit=12)
    with jax.named_scope("core_rows"):
        sib = core_swap(for_sib)
    half = ((width + EXTRA, rows), BF)
    full = ((YL, width + EXTRA, rows), BF)
    shape = [((rows, heads * hd), BF, None), ((n, rows), BF), eight, half, half]
    kernel = functools.partial(attend, heads, hd)
    attn_out, gt, sums, to_fwd, to_bwd = call(
        kernel, shape, qkv, wg, head_gains, d_out, w, limit=8
    )
    with jax.named_scope("core_grads"):
        gs = core_swap(gt)
    with jax.named_scope("z_relay1"):
        fwd, bwd = z_step(to_fwd, 1), z_step(to_bwd, -1)

    def relay(terms, at, fwd, bwd, *deps):
        kernel = functools.partial(relay_message, at)
        to_fwd, to_bwd = call(kernel, [full] * 2, terms, fwd, bwd, sums, deps=deps)
        return to_fwd, z_step(to_fwd, 1), z_step(to_bwd, -1)

    one, wide = ((main, width), BF), width * YL
    shape = [one, one, ((X, rest, width), BF), ((2, wide, rows), BF)]
    far_fwd, far_bwd, r_other, near_terms = call(first_terms, shape, own, sib, gt, gs, w)
    with jax.named_scope("x_main1"):
        w_fwd, w_bwd = x_step(far_fwd, 1), x_step(far_bwd, -1)
    with jax.named_scope("yh_rest"):
        r_got = yh_swap(r_other)
    with jax.named_scope("z_relay2"):
        sent, fwd, bwd = relay(near_terms, 0, fwd, bwd)
    shape = [((6, main, width), BF), ((X, rest, width), BF), ((5, wide, rows), BF)]
    w_near, r_own, terms = call(later_terms, shape, own, sib, gt, gs, w, deps=[sent])
    with jax.named_scope("x_main2"):
        message = ((YH, main, width), BF)
        to_fwd, to_bwd = call(main_message, [message] * 2, w_near, w_fwd, w_bwd)
        w_fwd, w_bwd = x_step(to_fwd, 1), x_step(to_bwd, -1)
    with jax.named_scope("z_relay3"):
        sent, fwd, bwd = relay(terms, 0, fwd, bwd, to_fwd)
    with jax.named_scope("z_relay4"):
        sent, fwd, bwd = relay(terms, 2, fwd, bwd)
    with jax.named_scope("x_rest1"):
        shape = [((rest // 2, width), BF)] * 2
        to_fwd, to_bwd = call(rest_first, shape, r_own, r_got, deps=[sent])
        r_fwd, r_bwd = x_step(to_fwd, 1), x_step(to_bwd, -1)
    with jax.named_scope("yh_main"):
        shape = [((main, width), F32), ((main, width), BF)]
        mine, other = call(main_swap, shape, w_near, w_fwd, w_bwd, deps=[to_fwd])
        got = yh_swap(other)
    with jax.named_scope("x_rest2"):
        shape = [((rest, width), BF)] * 2
        to_fwd, to_bwd = call(rest_second, shape, r_own, r_got, r_fwd, r_bwd, deps=[other])
        r_fwd, r_bwd = x_step(to_fwd, 1), x_step(to_bwd, -1)
    with jax.named_scope("y_tokens"):
        kernel = functools.partial(swap_message, 4)
        to_mine, to_other = call(kernel, [half] * 2, terms, fwd, bwd, sums, deps=[to_fwd])
        got_y = yl_swap(to_other)
    with jax.named_scope("weight_out"):
        shape = [((width, heads, n3), F32, None), ((8, 128), F32)]
        operands = [mine, got, r_own, r_got, r_fwd, r_bwd]
        grad_weight, done = call(finish_weight, shape, *operands, deps=[to_other])
    with jax.named_scope("tokens_out"):
        shape = [((rows, width), BF, None)]
        operands = [to_mine, got_y, tokens, gains, stats]
        grad_tokens = call(finish_tokens, shape, *operands, deps=[done])[0]
    return attn_out, grad_tokens, grad_weight


def solution(mesh):
    in_specs = (P("dp", "mp"), P(), P(None, "mp", None), P(), P(), P("dp", "mp"))
    out_specs = (P("dp", "mp"), P("dp", "mp"), P("dp", "mp", None))
    return jax.shard_map(local, mesh=mesh, in_specs=in_specs, out_specs=out_specs, check_vma=False)
```

```python
import functools
import jax
import jax.numpy as jnp
from jax import lax
from jax.experimental import pallas as pl
from jax.experimental.pallas import tpu as pltpu
from jax.sharding import PartitionSpec as P

EPSILON = 1e-06
Z, YL, X, YH, CORES = 8, 2, 4, 2, 2
BF, F32 = jnp.bfloat16, jnp.float32
MIB = 1 << 20
GROUP = 16
EXTRA = 16
FAR = Z // 2
COST = pl.CostEstimate(flops=1024, bytes_accessed=1024, transcendentals=0)


def z_step(values, d):
    pairs = [(z * YL + y, ((z + d) % Z) * YL + y) for z in range(Z) for y in range(YL)]
    return lax.ppermute(values, "mp", pairs)


def yl_swap(values):
    return lax.ppermute(values, "mp", [(i, i ^ 1) for i in range(Z * YL)])


def x_step(values, d):
    n = YH * CORES
    pairs = [(x * n + r, ((x + d) % X) * n + r) for x in range(X) for r in range(n)]
    return lax.ppermute(values, "dp", pairs)


def yh_swap(values):
    return lax.ppermute(values, "dp", [(i, i ^ 2) for i in range(X * YH * CORES)])


def core_swap(values):
    return lax.ppermute(values, "dp", [(i, i ^ 1) for i in range(X * YH * CORES)])


def z_index():
    return lax.axis_index("mp") // YL


def yl_index():
    return lax.rem(lax.axis_index("mp"), YL)


def x_index():
    return lax.axis_index("dp") // (YH * CORES)


def yh_index():
    return lax.rem(lax.axis_index("dp") // CORES, YH)


def core_index():
    return lax.rem(lax.axis_index("dp"), CORES)


def held(shape, dtype):
    return pltpu.VMEM(shape, dtype)


def call(kernel, out_shape, *args, deps=(), hbm=(), limit=6, scratch=()):
    vmem, anywhere = pl.BlockSpec(memory_space=pltpu.VMEM), pl.BlockSpec(memory_space=pl.ANY)
    specs = [anywhere if i in hbm else vmem for i in range(len(args))]
    count = len(args)
    name = getattr(kernel, "func", kernel).__name__

    def body(*refs):
        kernel(*refs[:count], *refs[count + len(deps) :])

    return pl.pallas_call(
        body,
        in_specs=specs + [anywhere] * len(deps),
        out_specs=[vmem] * len(out_shape),
        out_shape=[(jax.ShapeDtypeStruct if o[2:] else held)(o[0], o[1]) for o in out_shape],
        scratch_shapes=list(scratch),
        compiler_params=pltpu.CompilerParams(vmem_limit_bytes=limit * MIB),
        cost_estimate=COST,
        name=name,
    )(*args, *deps)


def tie(values, dep, limit):
    anywhere = pl.BlockSpec(memory_space=pl.ANY)
    count = len(values)
    return pl.pallas_call(
        lambda *refs: None,
        in_specs=[anywhere] * (count + 1),
        out_specs=[anywhere] * count,
        out_shape=[jax.ShapeDtypeStruct(v.shape, v.dtype) for v in values],
        input_output_aliases={i: i for i in range(count)},
        compiler_params=pltpu.CompilerParams(vmem_limit_bytes=limit * MIB),
        cost_estimate=COST,
        name="tie",
    )(*values, dep)


def hold(ref, out_ref):
    out_ref[...] = ref[...]


def pair(*refs):
    count = len(refs) // 3
    for i, out_ref in enumerate(refs[2 * count :]):
        out_ref[0] = refs[2 * i][...]
        out_ref[1] = refs[2 * i + 1][...]


def load(source, out_ref, sems):
    groups = out_ref.shape[0] // Z
    copies = []
    for i in range(Z):
        part = pl.ds(i * groups, groups)
        copies.append(pltpu.make_async_copy(source.at[part], out_ref.at[part], sems.at[i]))
        copies[-1].start()
    for copy in copies:
        copy.wait()


def gather_tokens(tokens, w_qkv, *early):
    other = yl_swap(tokens)
    own_up, own_down = z_step(tokens, 1), z_step(tokens, -1)
    tokens = call(hold, [(tokens.shape, BF)], tokens, deps=[*early, other])[0]
    other_up, other_down = z_step(other, 1), z_step(other, -1)
    blocks, shape = {}, ((YL, *tokens.shape), BF)
    blocks[Z - 1], blocks[1] = call(pair, [shape] * 2, own_up, other_up, own_down, other_down)
    blocks[0] = call(pair, [shape], tokens, other, deps=[blocks[1]])[0]
    w = w_qkv.reshape(-1, GROUP, *w_qkv.shape[1:]).swapaxes(1, 2)
    for s in range(2, FAR):
        blocks[Z - s] = z_step(blocks[Z - s + 1], 1)
        blocks[s] = z_step(blocks[s - 1], -1)
        if s == 2:
            blocks[Z - s], blocks[s] = tie([blocks[Z - s], blocks[s]], w, 46)
        if s == 3:
            out, sems = [(w.shape, BF)], [pltpu.SemaphoreType.DMA((Z,))]
            deps = [blocks[2]]
            w = call(load, out, w, deps=deps, hbm=[0], limit=46, scratch=sems)[0]
            blocks[s] = tie([blocks[s]], w, 1)[0]
    blocks[FAR] = z_step(blocks[FAR + 1], 1)
    return [blocks[d] for d in range(Z)], w, tokens


def repeat(count, body):
    def step(i, carry):
        body(i)
        return carry

    lax.fori_loop(0, count, step, 0)


def entry(values, i):
    result = values[-1]
    for at, value in reversed(list(enumerate(values[:-1]))):
        result = jnp.where(i == at, value, result)
    return result


def joined(w_ref):
    heads, columns = w_ref.shape[1], w_ref.shape[3]
    return jnp.concatenate([w_ref[:, h].reshape(-1, columns) for h in range(heads)], 1)


def gains_at(gain_ref, d):
    z, yl = lax.rem(z_index() + d, Z), yl_index()
    return [gain_ref[z * YL + y] for y in (yl, 1 - yl)]


def w_at(w_ref, d):
    z, yl = lax.rem(z_index() + d, Z), yl_index()
    groups = w_ref.shape[0] // (Z * YL)
    firsts = [(z * YL + y) * groups for y in (yl, 1 - yl)]
    return jnp.concatenate([joined(w_ref.at[pl.ds(f, groups)]) for f in firsts], 0)


CHUNKS = 4


def row_sums(blocks, rows):
    size, width = blocks[0][0, rows].shape
    acc = jnp.zeros((size, width), F32)
    acc2 = jnp.zeros((size, width), F32)
    for block in blocks:
        for r in range(YL):
            v = block[r, rows].astype(F32)
            acc = acc + v
            acc2 = acc2 + v * v
    return jnp.sum(acc, 1, keepdims=True), jnp.sum(acc2, 1, keepdims=True)


def lanes(first, second, third):
    lane = lax.broadcasted_iota(jnp.int32, (first.shape[0], 128), 1)
    return jnp.where(lane == 0, first, jnp.where(lane == 1, second, third))


def centred(block, shift, gains):
    return jnp.concatenate(
        [((block[r].astype(F32) - shift) * g).astype(BF) for r, g in enumerate(gains)], 1
    )


def project_near(*refs):
    *blocks, gain_ref, w_ref, part_ref, wg_ref, sums_ref = refs
    rows, width = blocks[0].shape[1:]

    def chunk(i):
        at = pl.ds(pl.multiple_of(i * (rows // CHUNKS), rows // CHUNKS), rows // CHUNKS)
        total, square = row_sums(blocks, at)
        sums_ref[at] = lanes(total, square, total / (len(blocks) * YL * width))

    repeat(CHUNKS, chunk)
    shift = sums_ref[:, 2:3]
    part_ref[...] = jnp.zeros_like(part_ref)
    wg_ref[...] = jnp.zeros_like(wg_ref)
    for d in range(Z):
        gains = gains_at(gain_ref, d)
        left = jnp.broadcast_to(jnp.concatenate(gains, 1), (16, width * YL)).astype(BF)
        if d == FAR:
            wg_ref[...] += dot_nn(left, w_at(w_ref, d))
            continue
        block = blocks[d if d < FAR else d - 1]
        left = jnp.concatenate([centred(block, shift, gains), left], 0)
        product = dot_nn(left, w_at(w_ref, d))
        part_ref[...] += product[:rows]
        wg_ref[...] += product[rows:]


def project(*refs):
    blocks = refs[:Z]
    gain_ref, w_ref, part_ref, wg_ref, sums_ref, qkv_ref, own_ref, sib_ref, stats_ref = refs[Z:-1]
    both_ref = refs[-1]
    rows, width = blocks[0].shape[1:]
    cols = width * Z * YL
    total, square = row_sums([blocks[FAR]], slice(None))
    mean = (total + sums_ref[:, 0:1]) / cols
    inv = lax.rsqrt((square + sums_ref[:, 1:2]) / cols - mean * mean + EPSILON)
    shift = sums_ref[:, 2:3]
    both_ref[...] = lanes(mean, inv, 0.0)
    stats_ref[...] = both_ref[...].T[:8]
    gains = gains_at(gain_ref, FAR)
    product = dot_nn(centred(blocks[FAR], shift, gains), w_at(w_ref, FAR))
    qkv_ref[...] = inv * (part_ref[...] + product - (mean - shift) * wg_ref[0:1])
    first = core_index() == yl_index()

    def chunk(i):
        at = pl.ds(pl.multiple_of(i * (rows // CHUNKS), rows // CHUNKS), rows // CHUNKS)
        mean, inv = both_ref[at, 0:1], both_ref[at, 1:2]
        for d in range(Z):
            zd = lax.rem(z_index() + d, Z)
            parts = [
                ((blocks[d][r, at].astype(F32) - mean) * inv * g).astype(BF)
                for r, g in enumerate(gains_at(gain_ref, d))
            ]
            own_ref[zd, at] = jnp.where(first, parts[0], parts[1])
            sib_ref[zd, at] = jnp.where(first, parts[1], parts[0])

    repeat(CHUNKS, chunk)


def dot_nt(a, b):
    return lax.dot_general(a, b, (((1,), (1,)), ((), ())), preferred_element_type=F32)


def dot_tn(a, b):
    return lax.dot_general(a, b, (((0,), (0,)), ((), ())), preferred_element_type=F32)


def dot_nn(a, b):
    return jnp.dot(a, b, preferred_element_type=F32)


def head_norm(values):
    centred = values - jnp.mean(values, -1, keepdims=True)
    inv = lax.rsqrt(jnp.mean(centred * centred, -1, keepdims=True) + EPSILON)
    return centred * inv, inv


def norm_back(grad, gain, unit, inv):
    scaled = grad * gain
    return inv * (
        scaled
        - jnp.mean(scaled, -1, keepdims=True)
        - unit * jnp.mean(scaled * unit, -1, keepdims=True)
    )


def pack(sums):
    high = sums.astype(BF).astype(F32)
    return jnp.concatenate([high, sums - high], 0).astype(BF)


def unpack(extra):
    wide = extra.astype(F32)
    half = wide.shape[0] // 2
    return wide[:half] + wide[half:]


def attend(heads, hd, qkv_ref, wg_ref, gains_ref, do_ref, w_ref, *outs):
    out_ref, gt_ref, sums_ref, fwd_ref, bwd_ref = outs
    scale = hd ** (-0.5)
    q_gain, k_gain = gains_ref[0:1], gains_ref[1:2]
    rows = qkv_ref.shape[0]
    acc_sum = jnp.zeros((rows, hd), F32)
    acc_cross = jnp.zeros((rows, hd), F32)
    for h in range(heads):
        base = h * 3 * hd
        q, k, v = (qkv_ref[:, base + i * hd : base + (i + 1) * hd] for i in range(3))
        q_unit, q_inv = head_norm(q)
        k_unit, k_inv = head_norm(k)
        q_half = (q_unit * q_gain).astype(BF)
        k_half = (k_unit * k_gain).astype(BF)
        v_half = v.astype(BF)
        d_out = do_ref[:, h * hd : (h + 1) * hd]
        exps = jnp.exp(dot_nt(q_half, k_half) * scale)
        probs = exps / jnp.sum(exps, -1, keepdims=True)
        probs_half = probs.astype(BF)
        out_ref[:, h * hd : (h + 1) * hd] = dot_nn(probs_half, v_half).astype(BF)
        grad_probs = dot_nt(d_out, v_half)
        grad_value = dot_tn(probs_half, d_out)
        inner = jnp.sum(probs * grad_probs, -1, keepdims=True)
        grad_scores = (probs * (grad_probs - inner) * scale).astype(BF)
        grad_q = norm_back(dot_nn(grad_scores, k_half), q_gain, q_unit, q_inv)
        grad_k = norm_back(dot_tn(grad_scores, q_half), k_gain, k_unit, k_inv)
        for i, (part, source) in enumerate(((grad_q, q), (grad_k, k), (grad_value, v))):
            cols = slice(base + i * hd, base + (i + 1) * hd)
            half = part.astype(BF)
            gt_ref[cols, :] = half.T
            wide = half.astype(F32)
            acc_sum = acc_sum + wide * wg_ref[0:1, cols]
            acc_cross = acc_cross + wide * source
    sums = jnp.sum(acc_sum, -1, keepdims=True)
    cross = jnp.sum(acc_cross, -1, keepdims=True)
    lane = lax.broadcasted_iota(jnp.int32, (rows, hd), 1)
    both = jnp.where(lane == 0, sums, jnp.where(lane == 1, cross, 0.0))
    sums = both.T[:8]
    sums_ref[...] = sums
    extra = pack(sums)
    width = fwd_ref.shape[0] - extra.shape[0]
    term = term_at(w_ref, gt_ref, FAR)
    for ref, part in ((fwd_ref, term[:width]), (bwd_ref, term[width:])):
        ref[:width] = part
        ref[width:] = extra


def term_at(w_ref, gt_ref, d):
    groups = w_ref.shape[0] // Z
    start = lax.rem(z_index() + d, Z) * groups
    return dot_nn(joined(w_ref.at[pl.ds(start, groups)]), gt_ref[...]).astype(BF)


def relay_message(at, terms_ref, f_ref, b_ref, sums_ref, fwd_ref, bwd_ref):
    width = terms_ref.shape[1] // YL
    sums = sums_ref[...]
    whole = len(f_ref.shape) == 3
    for i, (got, ref) in enumerate(((f_ref, fwd_ref), (b_ref, bwd_ref))):
        for y in range(YL):
            term = terms_ref[at + i, y * width : (y + 1) * width]
            if whole or y == i:
                source = got.at[y] if whole else got
                ref[y, :width] = (term.astype(F32) + source[:width].astype(F32)).astype(BF)
                ref[y, width:] = pack(unpack(source[width:]) + sums)
            else:
                ref[y, :width] = term
                ref[y, width:] = pack(sums)


def swap_message(at, terms_ref, f_ref, b_ref, sums_ref, mine_ref, other_ref):
    width = terms_ref.shape[1] // YL
    yl = yl_index()
    for ref, y in ((mine_ref, yl), (other_ref, 1 - yl)):
        term = terms_ref[at, pl.ds(pl.multiple_of(y * width, width), width)]
        ref[:width] = wide_sum(term, f_ref[y, :width], b_ref[y, :width]).astype(BF)
        ref[width:] = pack(unpack(f_ref[y, width:]) + unpack(b_ref[y, width:]) + sums_ref[...])


def finish_tokens(mine_ref, other_ref, tok_ref, gain_ref, stats_ref, out_ref):
    rows, width = tok_ref.shape
    cols = width * Z * YL
    grad = wide_sum(mine_ref[:width], other_ref[:width]).T
    sums = (unpack(mine_ref[width:]) + unpack(other_ref[width:])).T / cols
    stats = stats_ref[...].T
    inv = stats[:, 1:2]
    scaled = grad * gain_ref[lax.axis_index("mp")]
    unit = (tok_ref[...].astype(F32) - stats[:, 0:1]) * inv
    out_ref[...] = (inv * (scaled - sums[:, 0:1] - unit * sums[:, 1:2])).astype(BF)


REST_DXS = (2, 1, 3, 0)


def weight_term(dx, h, left, own_ref, sib_ref):
    block = lax.rem(x_index() + dx, X) * YH + h
    right = jnp.concatenate([own_ref[block], sib_ref[block]], 0)
    return dot_nn(left, right).astype(BF)


def left_at(gt_ref, gs_ref, start, size):
    return jnp.concatenate([gt_ref[start : start + size], gs_ref[start : start + size]], 1)


def first_terms(own_ref, sib_ref, gt_ref, gs_ref, w_ref, fwd_ref, bwd_ref, other_ref, terms_ref):
    main, rest = fwd_ref.shape[0], other_ref.shape[1]
    left = left_at(gt_ref, gs_ref, 0, main)
    fwd_ref[...] = weight_term(2, 0, left, own_ref, sib_ref)
    bwd_ref[...] = weight_term(2, 1, left, own_ref, sib_ref)
    left = left_at(gt_ref, gs_ref, main, rest)
    for i, dx in enumerate(REST_DXS):
        other_ref[i] = weight_term(dx, 1 - yh_index(), left, own_ref, sib_ref)
    for i, d in enumerate((3, 5)):
        terms_ref[i] = term_at(w_ref, gt_ref, d)


def later_terms(own_ref, sib_ref, gt_ref, gs_ref, w_ref, near_ref, same_ref, terms_ref):
    main, rest = near_ref.shape[1], same_ref.shape[1]

    def near(i):
        left = left_at(gt_ref, gs_ref, 0, main)
        dx = entry((1, 3, 0), i // YH)
        near_ref[i] = weight_term(dx, lax.rem(i, YH), left, own_ref, sib_ref)

    def same(i):
        left = left_at(gt_ref, gs_ref, main, rest)
        same_ref[i] = weight_term(entry(REST_DXS, i), yh_index(), left, own_ref, sib_ref)

    def term(i):
        terms_ref[i] = term_at(w_ref, gt_ref, entry((2, 6, 1, 7, 0), i))

    repeat(near_ref.shape[0], near)
    repeat(same_ref.shape[0], same)
    repeat(terms_ref.shape[0], term)


def wide_sum(*parts):
    total = parts[0].astype(F32)
    for part in parts[1:]:
        total = total + part.astype(F32)
    return total


def main_message(near_ref, f_ref, b_ref, fwd_ref, bwd_ref):
    fwd_ref[0] = wide_sum(near_ref[0], f_ref[...]).astype(BF)
    fwd_ref[1] = near_ref[1]
    bwd_ref[0] = near_ref[2]
    bwd_ref[1] = wide_sum(near_ref[3], b_ref[...]).astype(BF)


def main_swap(near_ref, f_ref, b_ref, mine_ref, other_ref):
    yh = yh_index()
    other = 1 - yh
    mine_ref[...] = wide_sum(near_ref[4 + yh], f_ref[yh], b_ref[yh])
    other_ref[...] = wide_sum(near_ref[4 + other], f_ref[other], b_ref[other]).astype(BF)


def rest_first(own_ref, got_ref, fwd_ref, bwd_ref):
    half = fwd_ref.shape[0]
    fwd_ref[...] = wide_sum(own_ref[0, :half], got_ref[0, :half]).astype(BF)
    bwd_ref[...] = wide_sum(own_ref[0, half:], got_ref[0, half:]).astype(BF)


def rest_second(own_ref, got_ref, f_ref, b_ref, fwd_ref, bwd_ref):
    half = f_ref.shape[0]
    fwd_ref[:half] = wide_sum(own_ref[1, :half], got_ref[1, :half], f_ref[...]).astype(BF)
    fwd_ref[half:] = wide_sum(own_ref[1, half:], got_ref[1, half:]).astype(BF)
    bwd_ref[:half] = wide_sum(own_ref[2, :half], got_ref[2, :half]).astype(BF)
    bwd_ref[half:] = wide_sum(own_ref[2, half:], got_ref[2, half:], b_ref[...]).astype(BF)


def finish_weight(mine_ref, got_ref, own_ref, other_ref, f_ref, b_ref, out_ref, done_ref):
    done_ref[...] = jnp.zeros_like(done_ref)
    main, n3 = mine_ref.shape[0], out_ref.shape[2]
    parts = [
        wide_sum(mine_ref[...], got_ref[...]),
        wide_sum(own_ref[3], other_ref[3], f_ref[...], b_ref[...]),
    ]
    whole = jnp.concatenate(parts, 0)
    for h in range(out_ref.shape[1]):
        out_ref[:, h, :] = whole[h * n3 : (h + 1) * n3].T


def local(tokens, ln_gain, w_qkv, q_gain, k_gain, d_out):
    rows, width = tokens.shape
    heads, n3 = w_qkv.shape[1:]
    n = heads * n3
    hd = n3 // 3
    main = n // 2
    rest = n - main
    gains = ln_gain.astype(F32).reshape(Z * YL, 1, width)
    head_gains = jnp.stack([q_gain, k_gain]).astype(F32)

    with jax.named_scope("gather"):
        blocks, w, tokens = gather_tokens(tokens, w_qkv, gains, head_gains)
    blocks_shape = ((Z, rows, width), BF)
    eight = ((8, rows), F32)
    qkv_shape = ((rows, n), F32)
    near = blocks[:FAR] + blocks[FAR + 1 :]
    shape = [qkv_shape, ((16, n), F32), ((rows, 128), F32)]
    part, wg, row_part = call(project_near, shape, *near, gains, w, limit=12)
    shape = [qkv_shape, blocks_shape, blocks_shape, eight]
    operands = [*blocks, gains, w, part, wg, row_part]
    scratch = [pltpu.VMEM((rows, 128), F32)]
    qkv, own, for_sib, stats = call(project, shape, *operands, limit=12, scratch=scratch)
    with jax.named_scope("core_rows"):
        sib = core_swap(for_sib)
    half = ((width + EXTRA, rows), BF)
    full = ((YL, width + EXTRA, rows), BF)
    shape = [((rows, heads * hd), BF, None), ((n, rows), BF), eight, half, half]
    kernel = functools.partial(attend, heads, hd)
    attn_out, gt, sums, to_fwd, to_bwd = call(
        kernel, shape, qkv, wg, head_gains, d_out, w, limit=8
    )
    with jax.named_scope("core_grads"):
        gs = core_swap(gt)
    with jax.named_scope("z_relay1"):
        fwd, bwd = z_step(to_fwd, 1), z_step(to_bwd, -1)

    def relay(terms, at, fwd, bwd, *deps):
        kernel = functools.partial(relay_message, at)
        to_fwd, to_bwd = call(kernel, [full] * 2, terms, fwd, bwd, sums, deps=deps)
        return to_fwd, z_step(to_fwd, 1), z_step(to_bwd, -1)

    one, wide = ((main, width), BF), width * YL
    shape = [one, one, ((X, rest, width), BF), ((2, wide, rows), BF)]
    far_fwd, far_bwd, r_other, near_terms = call(first_terms, shape, own, sib, gt, gs, w)
    with jax.named_scope("x_main1"):
        w_fwd, w_bwd = x_step(far_fwd, 1), x_step(far_bwd, -1)
    with jax.named_scope("yh_rest"):
        r_got = yh_swap(r_other)
    with jax.named_scope("z_relay2"):
        sent, fwd, bwd = relay(near_terms, 0, fwd, bwd)
    shape = [((6, main, width), BF), ((X, rest, width), BF), ((5, wide, rows), BF)]
    w_near, r_own, terms = call(later_terms, shape, own, sib, gt, gs, w, deps=[sent])
    with jax.named_scope("x_main2"):
        message = ((YH, main, width), BF)
        to_fwd, to_bwd = call(main_message, [message] * 2, w_near, w_fwd, w_bwd)
        w_fwd, w_bwd = x_step(to_fwd, 1), x_step(to_bwd, -1)
    with jax.named_scope("z_relay3"):
        sent, fwd, bwd = relay(terms, 0, fwd, bwd, to_fwd)
    with jax.named_scope("z_relay4"):
        sent, fwd, bwd = relay(terms, 2, fwd, bwd)
    with jax.named_scope("x_rest1"):
        shape = [((rest // 2, width), BF)] * 2
        to_fwd, to_bwd = call(rest_first, shape, r_own, r_got, deps=[sent])
        r_fwd, r_bwd = x_step(to_fwd, 1), x_step(to_bwd, -1)
    with jax.named_scope("yh_main"):
        shape = [((main, width), F32), ((main, width), BF)]
        mine, other = call(main_swap, shape, w_near, w_fwd, w_bwd, deps=[to_fwd])
        got = yh_swap(other)
    with jax.named_scope("x_rest2"):
        shape = [((rest, width), BF)] * 2
        to_fwd, to_bwd = call(rest_second, shape, r_own, r_got, r_fwd, r_bwd, deps=[other])
        r_fwd, r_bwd = x_step(to_fwd, 1), x_step(to_bwd, -1)
    with jax.named_scope("y_tokens"):
        kernel = functools.partial(swap_message, 4)
        to_mine, to_other = call(kernel, [half] * 2, terms, fwd, bwd, sums, deps=[to_fwd])
        got_y = yl_swap(to_other)
    with jax.named_scope("weight_out"):
        shape = [((width, heads, n3), F32, None), ((8, 128), F32)]
        operands = [mine, got, r_own, r_got, r_fwd, r_bwd]
        grad_weight, done = call(finish_weight, shape, *operands, deps=[to_other])
    with jax.named_scope("tokens_out"):
        shape = [((rows, width), BF, None)]
        operands = [to_mine, got_y, tokens, gains, stats]
        grad_tokens = call(finish_tokens, shape, *operands, deps=[done])[0]
    return attn_out, grad_tokens, grad_weight


def solution(mesh):
    in_specs = (P("dp", "mp"), P(), P(None, "mp", None), P(), P(), P("dp", "mp"))
    out_specs = (P("dp", "mp"), P("dp", "mp"), P("dp", "mp", None))
    return jax.shard_map(local, mesh=mesh, in_specs=in_specs, out_specs=out_specs, check_vma=False)
```

```python
import functools
import jax
import jax.numpy as jnp
from jax import lax
from jax.experimental import pallas as pl
from jax.experimental.pallas import tpu as pltpu
from jax.sharding import PartitionSpec as P

EPSILON = 1e-06
Z, YL, X, YH, CORES = 8, 2, 4, 2, 2
BF, F32 = jnp.bfloat16, jnp.float32
MIB = 1 << 20
GROUP = 16
EXTRA = 16
FAR = Z // 2
COST = pl.CostEstimate(flops=1024, bytes_accessed=1024, transcendentals=0)


def z_step(values, d):
    pairs = [(z * YL + y, ((z + d) % Z) * YL + y) for z in range(Z) for y in range(YL)]
    return lax.ppermute(values, "mp", pairs)


def yl_swap(values):
    return lax.ppermute(values, "mp", [(i, i ^ 1) for i in range(Z * YL)])


def x_step(values, d):
    n = YH * CORES
    pairs = [(x * n + r, ((x + d) % X) * n + r) for x in range(X) for r in range(n)]
    return lax.ppermute(values, "dp", pairs)


def yh_swap(values):
    return lax.ppermute(values, "dp", [(i, i ^ 2) for i in range(X * YH * CORES)])


def core_swap(values):
    return lax.ppermute(values, "dp", [(i, i ^ 1) for i in range(X * YH * CORES)])


def z_index():
    return lax.axis_index("mp") // YL


def yl_index():
    return lax.rem(lax.axis_index("mp"), YL)


def x_index():
    return lax.axis_index("dp") // (YH * CORES)


def yh_index():
    return lax.rem(lax.axis_index("dp") // CORES, YH)


def core_index():
    return lax.rem(lax.axis_index("dp"), CORES)


def held(shape, dtype):
    return pltpu.VMEM(shape, dtype)


def call(kernel, out_shape, *args, deps=(), hbm=(), limit=6, scratch=()):
    vmem, anywhere = pl.BlockSpec(memory_space=pltpu.VMEM), pl.BlockSpec(memory_space=pl.ANY)
    specs = [anywhere if i in hbm else vmem for i in range(len(args))]
    count = len(args)
    name = getattr(kernel, "func", kernel).__name__

    def body(*refs):
        kernel(*refs[:count], *refs[count + len(deps) :])

    return pl.pallas_call(
        body,
        in_specs=specs + [anywhere] * len(deps),
        out_specs=[vmem] * len(out_shape),
        out_shape=[(jax.ShapeDtypeStruct if o[2:] else held)(o[0], o[1]) for o in out_shape],
        scratch_shapes=list(scratch),
        compiler_params=pltpu.CompilerParams(vmem_limit_bytes=limit * MIB),
        cost_estimate=COST,
        name=name,
    )(*args, *deps)


def tie(values, dep, limit):
    anywhere = pl.BlockSpec(memory_space=pl.ANY)
    count = len(values)
    return pl.pallas_call(
        lambda *refs: None,
        in_specs=[anywhere] * (count + 1),
        out_specs=[anywhere] * count,
        out_shape=[jax.ShapeDtypeStruct(v.shape, v.dtype) for v in values],
        input_output_aliases={i: i for i in range(count)},
        compiler_params=pltpu.CompilerParams(vmem_limit_bytes=limit * MIB),
        cost_estimate=COST,
        name="tie",
    )(*values, dep)


def hold(ref, out_ref):
    out_ref[...] = ref[...]


def pair(*refs):
    count = len(refs) // 3
    for i, out_ref in enumerate(refs[2 * count :]):
        out_ref[0] = refs[2 * i][...]
        out_ref[1] = refs[2 * i + 1][...]


def load(source, out_ref, sems):
    groups = out_ref.shape[0] // Z
    copies = []
    for i in range(Z):
        part = pl.ds(i * groups, groups)
        copies.append(pltpu.make_async_copy(source.at[part], out_ref.at[part], sems.at[i]))
        copies[-1].start()
    for copy in copies:
        copy.wait()


def gather_tokens(tokens, w_qkv, *early):
    other = yl_swap(tokens)
    own_up, own_down = z_step(tokens, 1), z_step(tokens, -1)
    tokens = call(hold, [(tokens.shape, BF)], tokens, deps=[*early, other])[0]
    other_up, other_down = z_step(other, 1), z_step(other, -1)
    blocks, shape = {}, ((YL, *tokens.shape), BF)
    blocks[Z - 1], blocks[1] = call(pair, [shape] * 2, own_up, other_up, own_down, other_down)
    blocks[0] = call(pair, [shape], tokens, other, deps=[blocks[1]])[0]
    w = w_qkv.reshape(-1, GROUP, *w_qkv.shape[1:]).swapaxes(1, 2)
    for s in range(2, FAR):
        blocks[Z - s] = z_step(blocks[Z - s + 1], 1)
        blocks[s] = z_step(blocks[s - 1], -1)
        if s == 2:
            blocks[Z - s], blocks[s] = tie([blocks[Z - s], blocks[s]], w, 46)
        if s == 3:
            out, sems = [(w.shape, BF)], [pltpu.SemaphoreType.DMA((Z,))]
            deps = [blocks[2]]
            w = call(load, out, w, deps=deps, hbm=[0], limit=44, scratch=sems)[0]
            blocks[s] = tie([blocks[s]], w, 1)[0]
    blocks[FAR] = z_step(blocks[FAR + 1], 1)
    return [blocks[d] for d in range(Z)], w, tokens


def repeat(count, body):
    def step(i, carry):
        body(i)
        return carry

    lax.fori_loop(0, count, step, 0)


def entry(values, i):
    result = values[-1]
    for at, value in reversed(list(enumerate(values[:-1]))):
        result = jnp.where(i == at, value, result)
    return result


def joined(w_ref):
    heads, columns = w_ref.shape[1], w_ref.shape[3]
    return jnp.concatenate([w_ref[:, h].reshape(-1, columns) for h in range(heads)], 1)


def gains_at(gain_ref, d):
    z, yl = lax.rem(z_index() + d, Z), yl_index()
    return [gain_ref[z * YL + y] for y in (yl, 1 - yl)]


def w_at(w_ref, d):
    z, yl = lax.rem(z_index() + d, Z), yl_index()
    groups = w_ref.shape[0] // (Z * YL)
    firsts = [(z * YL + y) * groups for y in (yl, 1 - yl)]
    return jnp.concatenate([joined(w_ref.at[pl.ds(f, groups)]) for f in firsts], 0)


CHUNKS = 4


def row_sums(blocks, rows):
    size, width = blocks[0][0, rows].shape
    acc = jnp.zeros((size, width), F32)
    acc2 = jnp.zeros((size, width), F32)
    for block in blocks:
        for r in range(YL):
            v = block[r, rows].astype(F32)
            acc = acc + v
            acc2 = acc2 + v * v
    return jnp.sum(acc, 1, keepdims=True), jnp.sum(acc2, 1, keepdims=True)


def lanes(first, second, third):
    lane = lax.broadcasted_iota(jnp.int32, (first.shape[0], 128), 1)
    return jnp.where(lane == 0, first, jnp.where(lane == 1, second, third))


def centred(block, shift, gains):
    return jnp.concatenate(
        [((block[r].astype(F32) - shift) * g).astype(BF) for r, g in enumerate(gains)], 1
    )


def project_near(*refs):
    *blocks, gain_ref, w_ref, part_ref, wg_ref, sums_ref = refs
    rows, width = blocks[0].shape[1:]

    def chunk(i):
        at = pl.ds(pl.multiple_of(i * (rows // CHUNKS), rows // CHUNKS), rows // CHUNKS)
        total, square = row_sums(blocks, at)
        sums_ref[at] = lanes(total, square, total / (len(blocks) * YL * width))

    repeat(CHUNKS, chunk)
    shift = sums_ref[:, 2:3]
    part_ref[...] = jnp.zeros_like(part_ref)
    wg_ref[...] = jnp.zeros_like(wg_ref)
    for d in range(Z):
        gains = gains_at(gain_ref, d)
        left = jnp.broadcast_to(jnp.concatenate(gains, 1), (16, width * YL)).astype(BF)
        if d == FAR:
            wg_ref[...] += dot_nn(left, w_at(w_ref, d))
            continue
        block = blocks[d if d < FAR else d - 1]
        left = jnp.concatenate([centred(block, shift, gains), left], 0)
        product = dot_nn(left, w_at(w_ref, d))
        part_ref[...] += product[:rows]
        wg_ref[...] += product[rows:]


def project(*refs):
    blocks = refs[:Z]
    gain_ref, w_ref, part_ref, wg_ref, sums_ref, qkv_ref, own_ref, sib_ref, stats_ref = refs[Z:-1]
    both_ref = refs[-1]
    rows, width = blocks[0].shape[1:]
    cols = width * Z * YL
    total, square = row_sums([blocks[FAR]], slice(None))
    mean = (total + sums_ref[:, 0:1]) / cols
    inv = lax.rsqrt((square + sums_ref[:, 1:2]) / cols - mean * mean + EPSILON)
    shift = sums_ref[:, 2:3]
    both_ref[...] = lanes(mean, inv, 0.0)
    stats_ref[...] = both_ref[...].T[:8]
    gains = gains_at(gain_ref, FAR)
    product = dot_nn(centred(blocks[FAR], shift, gains), w_at(w_ref, FAR))
    qkv_ref[...] = inv * (part_ref[...] + product - (mean - shift) * wg_ref[0:1])
    first = core_index() == yl_index()

    def chunk(i):
        at = pl.ds(pl.multiple_of(i * (rows // CHUNKS), rows // CHUNKS), rows // CHUNKS)
        mean, inv = both_ref[at, 0:1], both_ref[at, 1:2]
        for d in range(Z):
            zd = lax.rem(z_index() + d, Z)
            parts = [
                ((blocks[d][r, at].astype(F32) - mean) * inv * g).astype(BF)
                for r, g in enumerate(gains_at(gain_ref, d))
            ]
            own_ref[zd, at] = jnp.where(first, parts[0], parts[1])
            sib_ref[zd, at] = jnp.where(first, parts[1], parts[0])

    repeat(CHUNKS, chunk)


def dot_nt(a, b):
    return lax.dot_general(a, b, (((1,), (1,)), ((), ())), preferred_element_type=F32)


def dot_tn(a, b):
    return lax.dot_general(a, b, (((0,), (0,)), ((), ())), preferred_element_type=F32)


def dot_nn(a, b):
    return jnp.dot(a, b, preferred_element_type=F32)


def head_norm(values):
    centred = values - jnp.mean(values, -1, keepdims=True)
    inv = lax.rsqrt(jnp.mean(centred * centred, -1, keepdims=True) + EPSILON)
    return centred * inv, inv


def norm_back(grad, gain, unit, inv):
    scaled = grad * gain
    return inv * (
        scaled
        - jnp.mean(scaled, -1, keepdims=True)
        - unit * jnp.mean(scaled * unit, -1, keepdims=True)
    )


def pack(sums):
    high = sums.astype(BF).astype(F32)
    return jnp.concatenate([high, sums - high], 0).astype(BF)


def unpack(extra):
    wide = extra.astype(F32)
    half = wide.shape[0] // 2
    return wide[:half] + wide[half:]


def attend(heads, hd, qkv_ref, wg_ref, gains_ref, do_ref, w_ref, *outs):
    out_ref, gt_ref, sums_ref, fwd_ref, bwd_ref = outs
    scale = hd ** (-0.5)
    q_gain, k_gain = gains_ref[0:1], gains_ref[1:2]
    rows = qkv_ref.shape[0]
    acc_sum = jnp.zeros((rows, hd), F32)
    acc_cross = jnp.zeros((rows, hd), F32)
    for h in range(heads):
        base = h * 3 * hd
        q, k, v = (qkv_ref[:, base + i * hd : base + (i + 1) * hd] for i in range(3))
        q_unit, q_inv = head_norm(q)
        k_unit, k_inv = head_norm(k)
        q_half = (q_unit * q_gain).astype(BF)
        k_half = (k_unit * k_gain).astype(BF)
        v_half = v.astype(BF)
        d_out = do_ref[:, h * hd : (h + 1) * hd]
        exps = jnp.exp(dot_nt(q_half, k_half) * scale)
        probs = exps / jnp.sum(exps, -1, keepdims=True)
        probs_half = probs.astype(BF)
        out_ref[:, h * hd : (h + 1) * hd] = dot_nn(probs_half, v_half).astype(BF)
        grad_probs = dot_nt(d_out, v_half)
        grad_value = dot_tn(probs_half, d_out)
        inner = jnp.sum(probs * grad_probs, -1, keepdims=True)
        grad_scores = (probs * (grad_probs - inner) * scale).astype(BF)
        grad_q = norm_back(dot_nn(grad_scores, k_half), q_gain, q_unit, q_inv)
        grad_k = norm_back(dot_tn(grad_scores, q_half), k_gain, k_unit, k_inv)
        for i, (part, source) in enumerate(((grad_q, q), (grad_k, k), (grad_value, v))):
            cols = slice(base + i * hd, base + (i + 1) * hd)
            half = part.astype(BF)
            gt_ref[cols, :] = half.T
            wide = half.astype(F32)
            acc_sum = acc_sum + wide * wg_ref[0:1, cols]
            acc_cross = acc_cross + wide * source
    sums = jnp.sum(acc_sum, -1, keepdims=True)
    cross = jnp.sum(acc_cross, -1, keepdims=True)
    lane = lax.broadcasted_iota(jnp.int32, (rows, hd), 1)
    both = jnp.where(lane == 0, sums, jnp.where(lane == 1, cross, 0.0))
    sums = both.T[:8]
    sums_ref[...] = sums
    extra = pack(sums)
    width = fwd_ref.shape[0] - extra.shape[0]
    term = term_at(w_ref, gt_ref, FAR)
    for ref, part in ((fwd_ref, term[:width]), (bwd_ref, term[width:])):
        ref[:width] = part
        ref[width:] = extra


def term_at(w_ref, gt_ref, d):
    groups = w_ref.shape[0] // Z
    start = lax.rem(z_index() + d, Z) * groups
    return dot_nn(joined(w_ref.at[pl.ds(start, groups)]), gt_ref[...]).astype(BF)


def relay_message(at, terms_ref, f_ref, b_ref, sums_ref, fwd_ref, bwd_ref):
    width = terms_ref.shape[1] // YL
    sums = sums_ref[...]
    whole = len(f_ref.shape) == 3
    for i, (got, ref) in enumerate(((f_ref, fwd_ref), (b_ref, bwd_ref))):
        for y in range(YL):
            term = terms_ref[at + i, y * width : (y + 1) * width]
            if whole or y == i:
                source = got.at[y] if whole else got
                ref[y, :width] = (term.astype(F32) + source[:width].astype(F32)).astype(BF)
                ref[y, width:] = pack(unpack(source[width:]) + sums)
            else:
                ref[y, :width] = term
                ref[y, width:] = pack(sums)


def swap_message(at, terms_ref, f_ref, b_ref, sums_ref, mine_ref, other_ref):
    width = terms_ref.shape[1] // YL
    yl = yl_index()
    for ref, y in ((mine_ref, yl), (other_ref, 1 - yl)):
        term = terms_ref[at, pl.ds(pl.multiple_of(y * width, width), width)]
        ref[:width] = wide_sum(term, f_ref[y, :width], b_ref[y, :width]).astype(BF)
        ref[width:] = pack(unpack(f_ref[y, width:]) + unpack(b_ref[y, width:]) + sums_ref[...])


def finish_tokens(mine_ref, other_ref, tok_ref, gain_ref, stats_ref, out_ref):
    rows, width = tok_ref.shape
    cols = width * Z * YL
    grad = wide_sum(mine_ref[:width], other_ref[:width]).T
    sums = (unpack(mine_ref[width:]) + unpack(other_ref[width:])).T / cols
    stats = stats_ref[...].T
    inv = stats[:, 1:2]
    scaled = grad * gain_ref[lax.axis_index("mp")]
    unit = (tok_ref[...].astype(F32) - stats[:, 0:1]) * inv
    out_ref[...] = (inv * (scaled - sums[:, 0:1] - unit * sums[:, 1:2])).astype(BF)


REST_DXS = (2, 1, 3, 0)


def weight_term(dx, h, left, own_ref, sib_ref):
    block = lax.rem(x_index() + dx, X) * YH + h
    right = jnp.concatenate([own_ref[block], sib_ref[block]], 0)
    return dot_nn(left, right).astype(BF)


def left_at(gt_ref, gs_ref, start, size):
    return jnp.concatenate([gt_ref[start : start + size], gs_ref[start : start + size]], 1)


def first_terms(own_ref, sib_ref, gt_ref, gs_ref, w_ref, fwd_ref, bwd_ref, other_ref, terms_ref):
    main, rest = fwd_ref.shape[0], other_ref.shape[1]
    left = left_at(gt_ref, gs_ref, 0, main)
    fwd_ref[...] = weight_term(2, 0, left, own_ref, sib_ref)
    bwd_ref[...] = weight_term(2, 1, left, own_ref, sib_ref)
    left = left_at(gt_ref, gs_ref, main, rest)
    for i, dx in enumerate(REST_DXS):
        other_ref[i] = weight_term(dx, 1 - yh_index(), left, own_ref, sib_ref)
    for i, d in enumerate((3, 5)):
        terms_ref[i] = term_at(w_ref, gt_ref, d)


def later_terms(own_ref, sib_ref, gt_ref, gs_ref, w_ref, near_ref, same_ref, terms_ref):
    main, rest = near_ref.shape[1], same_ref.shape[1]

    def near(i):
        left = left_at(gt_ref, gs_ref, 0, main)
        dx = entry((1, 3, 0), i // YH)
        near_ref[i] = weight_term(dx, lax.rem(i, YH), left, own_ref, sib_ref)

    def same(i):
        left = left_at(gt_ref, gs_ref, main, rest)
        same_ref[i] = weight_term(entry(REST_DXS, i), yh_index(), left, own_ref, sib_ref)

    def term(i):
        terms_ref[i] = term_at(w_ref, gt_ref, entry((2, 6, 1, 7, 0), i))

    repeat(near_ref.shape[0], near)
    repeat(same_ref.shape[0], same)
    repeat(terms_ref.shape[0], term)


def wide_sum(*parts):
    total = parts[0].astype(F32)
    for part in parts[1:]:
        total = total + part.astype(F32)
    return total


def main_message(near_ref, f_ref, b_ref, fwd_ref, bwd_ref):
    fwd_ref[0] = wide_sum(near_ref[0], f_ref[...]).astype(BF)
    fwd_ref[1] = near_ref[1]
    bwd_ref[0] = near_ref[2]
    bwd_ref[1] = wide_sum(near_ref[3], b_ref[...]).astype(BF)


def main_swap(near_ref, f_ref, b_ref, mine_ref, other_ref):
    yh = yh_index()
    other = 1 - yh
    mine_ref[...] = wide_sum(near_ref[4 + yh], f_ref[yh], b_ref[yh])
    other_ref[...] = wide_sum(near_ref[4 + other], f_ref[other], b_ref[other]).astype(BF)


def rest_first(own_ref, got_ref, fwd_ref, bwd_ref):
    half = fwd_ref.shape[0]
    fwd_ref[...] = wide_sum(own_ref[0, :half], got_ref[0, :half]).astype(BF)
    bwd_ref[...] = wide_sum(own_ref[0, half:], got_ref[0, half:]).astype(BF)


def rest_second(own_ref, got_ref, f_ref, b_ref, fwd_ref, bwd_ref):
    half = f_ref.shape[0]
    fwd_ref[:half] = wide_sum(own_ref[1, :half], got_ref[1, :half], f_ref[...]).astype(BF)
    fwd_ref[half:] = wide_sum(own_ref[1, half:], got_ref[1, half:]).astype(BF)
    bwd_ref[:half] = wide_sum(own_ref[2, :half], got_ref[2, :half]).astype(BF)
    bwd_ref[half:] = wide_sum(own_ref[2, half:], got_ref[2, half:], b_ref[...]).astype(BF)


def finish_main(mine_ref, got_ref, out_ref):
    out_ref[...] = wide_sum(mine_ref[...], got_ref[...]).T


def finish_weight(main_ref, own_ref, other_ref, f_ref, b_ref, out_ref, done_ref):
    done_ref[...] = jnp.zeros_like(done_ref)
    n3 = out_ref.shape[2]
    rest = wide_sum(own_ref[3], other_ref[3], f_ref[...], b_ref[...]).T
    whole = jnp.concatenate([main_ref[...], rest], 1)
    for h in range(out_ref.shape[1]):
        out_ref[:, h, :] = whole[:, h * n3 : (h + 1) * n3]


def local(tokens, ln_gain, w_qkv, q_gain, k_gain, d_out):
    rows, width = tokens.shape
    heads, n3 = w_qkv.shape[1:]
    n = heads * n3
    hd = n3 // 3
    main = n // 2
    rest = n - main
    gains = ln_gain.astype(F32).reshape(Z * YL, 1, width)
    head_gains = jnp.stack([q_gain, k_gain]).astype(F32)

    with jax.named_scope("gather"):
        blocks, w, tokens = gather_tokens(tokens, w_qkv, gains, head_gains)
    blocks_shape = ((Z, rows, width), BF)
    eight = ((8, rows), F32)
    qkv_shape = ((rows, n), F32)
    near = blocks[:FAR] + blocks[FAR + 1 :]
    shape = [qkv_shape, ((16, n), F32), ((rows, 128), F32)]
    part, wg, row_part = call(project_near, shape, *near, gains, w, limit=12)
    shape = [qkv_shape, blocks_shape, blocks_shape, eight]
    operands = [*blocks, gains, w, part, wg, row_part]
    scratch = [pltpu.VMEM((rows, 128), F32)]
    qkv, own, for_sib, stats = call(project, shape, *operands, limit=12, scratch=scratch)
    with jax.named_scope("core_rows"):
        sib = core_swap(for_sib)
    half = ((width + EXTRA, rows), BF)
    full = ((YL, width + EXTRA, rows), BF)
    shape = [((rows, heads * hd), BF, None), ((n, rows), BF), eight, half, half]
    kernel = functools.partial(attend, heads, hd)
    attn_out, gt, sums, to_fwd, to_bwd = call(
        kernel, shape, qkv, wg, head_gains, d_out, w, limit=8
    )
    with jax.named_scope("core_grads"):
        gs = core_swap(gt)
    with jax.named_scope("z_relay1"):
        fwd, bwd = z_step(to_fwd, 1), z_step(to_bwd, -1)

    def relay(terms, at, fwd, bwd, *deps):
        kernel = functools.partial(relay_message, at)
        to_fwd, to_bwd = call(kernel, [full] * 2, terms, fwd, bwd, sums, deps=deps)
        return to_fwd, z_step(to_fwd, 1), z_step(to_bwd, -1)

    one, wide = ((main, width), BF), width * YL
    shape = [one, one, ((X, rest, width), BF), ((2, wide, rows), BF)]
    far_fwd, far_bwd, r_other, near_terms = call(first_terms, shape, own, sib, gt, gs, w)
    with jax.named_scope("x_main1"):
        w_fwd, w_bwd = x_step(far_fwd, 1), x_step(far_bwd, -1)
    with jax.named_scope("yh_rest"):
        r_got = yh_swap(r_other)
    with jax.named_scope("z_relay2"):
        sent, fwd, bwd = relay(near_terms, 0, fwd, bwd)
    shape = [((6, main, width), BF), ((X, rest, width), BF), ((5, wide, rows), BF)]
    w_near, r_own, terms = call(later_terms, shape, own, sib, gt, gs, w, deps=[sent])
    with jax.named_scope("x_main2"):
        message = ((YH, main, width), BF)
        to_fwd, to_bwd = call(main_message, [message] * 2, w_near, w_fwd, w_bwd)
        w_fwd, w_bwd = x_step(to_fwd, 1), x_step(to_bwd, -1)
    with jax.named_scope("z_relay3"):
        sent, fwd, bwd = relay(terms, 0, fwd, bwd, to_fwd)
    with jax.named_scope("z_relay4"):
        sent, fwd, bwd = relay(terms, 2, fwd, bwd)
    with jax.named_scope("x_rest1"):
        shape = [((rest // 2, width), BF)] * 2
        to_fwd, to_bwd = call(rest_first, shape, r_own, r_got, deps=[sent])
        r_fwd, r_bwd = x_step(to_fwd, 1), x_step(to_bwd, -1)
    with jax.named_scope("yh_main"):
        shape = [((main, width), F32), ((main, width), BF)]
        mine, other = call(main_swap, shape, w_near, w_fwd, w_bwd, deps=[to_fwd])
        got = yh_swap(other)
    with jax.named_scope("x_rest2"):
        shape = [((rest, width), BF)] * 2
        to_fwd, to_bwd = call(rest_second, shape, r_own, r_got, r_fwd, r_bwd, deps=[other])
        r_fwd, r_bwd = x_step(to_fwd, 1), x_step(to_bwd, -1)
    with jax.named_scope("y_tokens"):
        kernel = functools.partial(swap_message, 4)
        to_mine, to_other = call(kernel, [half] * 2, terms, fwd, bwd, sums, deps=[to_fwd])
        got_y = yl_swap(to_other)
    with jax.named_scope("weight_out"):
        shape = [((width, heads, n3), F32, None), ((8, 128), F32)]
        main_out = call(finish_main, [((width, main), F32)], mine, got, deps=[to_other])[0]
        operands = [main_out, r_own, r_got, r_fwd, r_bwd]
        grad_weight, done = call(finish_weight, shape, *operands, deps=[to_other])
    with jax.named_scope("tokens_out"):
        shape = [((rows, width), BF, None)]
        operands = [to_mine, got_y, tokens, gains, stats]
        grad_tokens = call(finish_tokens, shape, *operands, deps=[done])[0]
    return attn_out, grad_tokens, grad_weight


def solution(mesh):
    in_specs = (P("dp", "mp"), P(), P(None, "mp", None), P(), P(), P("dp", "mp"))
    out_specs = (P("dp", "mp"), P("dp", "mp"), P("dp", "mp", None))
    return jax.shard_map(local, mesh=mesh, in_specs=in_specs, out_specs=out_specs, check_vma=False)
```
